128 devices in a mesh: tm: 16 (over x, z), space: 8 (over y, core).
Axes of the slice: x: 4, y: 4, z: 4, core: 2. Of those that a mesh axis runs over, the one named last changes fastest.
Arguments:
- source: float32 [32, 16, 256, 256], P('tm', 'space'), may hold values from -6 to 6
- start_field: float32 [16, 256, 256], P('space'), may hold values from -6 to 6
- last_guess: float32 [16, 256, 256], P('space'), may hold values from -6 to 6
- classes: int32 [16, 256, 256], P('space'), may hold values from 0 to 7
- conductivity: float32 [8], replicated, may hold values from 0.5 to 2
- alpha_num: int32 [1], replicated, may hold values from 4 to 16
Outputs:
- next_iterate: float32 [32, 16, 256, 256], P('tm', 'space')
The draws below stay inside these ranges and needn't reach their ends.
Inputs may be any that keep to these rules, and one draw needn't show every extreme that they name: `classes`: each cell's class indexes the conductivity table. The circulant parameter is alpha_num / 32.
All inputs are finite; a program needn't handle non-finite values.
Results may differ from the reference program's by a relative error of at most 0.00014.
Values sent between devices are 32-bit elements; how exact they have to be, the bound alone decides.
A program may use at most 128 MiB of HBM per device.

```python
import math
import jax
import jax.numpy as jnp
from jax import lax

NX = 256
NY = 256
CHEB = 8
CLASSES = 8
STEPS = 32
NZ = 16


def place_ends(result, stream_key, least, high):
    index_at = [jax.random.randint(jax.random.fold_in(stream_key, axis), (), 0, length) for axis, length in enumerate(result.shape)]
    main_axis = result.shape.index(max(result.shape))
    beside = index_at[:main_axis] + [(index_at[main_axis] + 1) % result.shape[main_axis]] + index_at[main_axis + 1:]
    return result.at[tuple(index_at)].set(least).at[tuple(beside)].set(high)


def shard_levels(rng, extent, pieces, least, high):
    def one(axis_at, parts):
        steps = jax.random.uniform(jax.random.fold_in(jax.random.fold_in(rng, 6), axis_at), (parts,), jnp.float32, least / len(pieces), high / len(pieces))
        return jnp.repeat(jnp.exp(steps), extent[axis_at] // parts).reshape((-1,) + (1,) * (len(extent) - axis_at - 1))

    loudness = one(*pieces[0])
    for cut in pieces[1:]:
        loudness = loudness * one(*cut)
    return loudness


def gaussian(rng, extent, deviation, limit, split=(), kind=jnp.bfloat16):
    values = deviation * jax.random.normal(rng, extent, jnp.float32)
    if split:
        values = values * shard_levels(rng, extent, split, -0.22, 0.18)
    return jnp.clip(values, -limit, limit).astype(kind)


def setup_inputs(seed: int = 0) -> dict:
    seeds = jax.random.split(jax.random.key(seed), 7)
    source = gaussian(seeds[0], (STEPS, NZ, NX, NY), 1.0, 6.0, ((0, 16), (1, 8)), jnp.float32)
    start_field = gaussian(seeds[1], (NZ, NX, NY), 1.0, 6.0, ((0, 8),), jnp.float32)
    last_guess = gaussian(seeds[2], (NZ, NX, NY), 1.0, 6.0, ((0, 8),), jnp.float32)
    classes = place_ends(jax.random.randint(seeds[3], (NZ, NX, NY), 0, CLASSES), jax.random.fold_in(seeds[3], 1), 0, CLASSES - 1).astype(jnp.int32)
    conductivity = jnp.clip(jnp.exp(jax.random.uniform(seeds[4], (CLASSES,), jnp.float32, math.log(0.5), math.log(2.0))), 0.5, 2.0)
    alpha_num = jax.random.randint(seeds[5], (1,), 4, 17).astype(jnp.int32)
    return dict(source=source, start_field=start_field, last_guess=last_guess, classes=classes, conductivity=conductivity, alpha_num=alpha_num)


HALF_SPAN = 12.0


def face_weights(padded):
    core = padded[1:-1, 1:-1, 1:-1]
    return (0.5 * (core + padded[2:, 1:-1, 1:-1]), 0.5 * (core + padded[:-2, 1:-1, 1:-1]),
            0.5 * (core + padded[1:-1, 2:, 1:-1]), 0.5 * (core + padded[1:-1, :-2, 1:-1]),
            0.5 * (core + padded[1:-1, 1:-1, 2:]), 0.5 * (core + padded[1:-1, 1:-1, :-2]))


def stiffness(field, faces):
    padded = jnp.pad(field, 1)
    total = faces[0] + faces[1] + faces[2] + faces[3] + faces[4] + faces[5]
    beside = faces[0] * padded[2:, 1:-1, 1:-1] + faces[1] * padded[:-2, 1:-1, 1:-1]
    beside = beside + faces[2] * padded[1:-1, 2:, 1:-1] + faces[3] * padded[1:-1, :-2, 1:-1]
    beside = beside + faces[4] * padded[1:-1, 1:-1, 2:] + faces[5] * padded[1:-1, 1:-1, :-2]
    return total * field - beside


def reference(source, start_field, last_guess, classes, conductivity, alpha_num):
    alpha = alpha_num[0].astype(jnp.float32) / 32.0
    log_alpha = jnp.log(alpha)
    times = jnp.arange(STEPS).astype(jnp.float32)
    scale = jnp.exp(log_alpha * times / STEPS)
    kappa = conductivity[classes]
    faces = face_weights(jnp.pad(kappa, 1))
    rhs = source.at[0].add(start_field - alpha * last_guess)
    weighted = rhs * scale[:, None, None, None]
    spectrum = jnp.fft.fft(weighted, axis=0)
    ratio = jnp.exp(log_alpha / STEPS)
    lam = 1.0 - ratio * jnp.exp(-2j * jnp.pi * times / STEPS)

    def solve_one(pair):
        right, shift = pair
        center = shift + HALF_SPAN
        sigma = center / HALF_SPAN
        rho = 1.0 / sigma
        direction = right / center
        solution = direction
        residual = right
        for sweep in range(CHEB):
            residual = residual - (shift * direction + stiffness(direction, faces))
            rho_next = 1.0 / (2.0 * sigma - rho)
            direction = (rho_next * rho) * direction + (2.0 * rho_next / HALF_SPAN) * residual
            solution = solution + direction
            rho = rho_next
        return solution

    solved = lax.map(solve_one, (spectrum, lam))
    back = jnp.real(jnp.fft.ifft(solved, axis=0))
    return (back * jnp.exp(-log_alpha * times / STEPS)[:, None, None, None]).astype(jnp.float32)
```

```python
import jax
import jax.numpy as jnp
from jax import lax
from jax.experimental import pallas as pl
from jax.experimental.pallas import tpu as pltpu
from jax.sharding import PartitionSpec as P

MESH = pl.DeviceIdType.MESH


def exchange_kernel(x_ref, o_ref, send, recv):
    tm = lax.axis_index("tm")
    sp = lax.axis_index("space")
    me = tm * 8 + sp
    bar = pltpu.get_barrier_semaphore()

    def greet(k, carry):
        t = (me + k) % 128
        pl.semaphore_signal(bar, inc=1, device_id=(t // 8, t % 8), device_id_type=MESH)
        return carry

    lax.fori_loop(1, 128, greet, 0)
    o_ref[me] = x_ref[me]
    pl.semaphore_wait(bar, 127)

    def go(k, carry):
        kk = (k * 37) % 128
        t0 = (tm // 4 + kk // 32) % 4 * 4 + (tm + kk // 8) % 4
        t1 = (sp // 2 + kk // 2) % 4 * 2 + (sp + kk) % 2
        pltpu.make_async_remote_copy(
            src_ref=x_ref.at[t0 * 8 + t1],
            dst_ref=o_ref.at[me],
            send_sem=send,
            recv_sem=recv,
            device_id=(t0, t1),
            device_id_type=MESH,
        ).start()
        return carry

    lax.fori_loop(1, 128, go, 0)
    rest = x_ref.at[pl.ds(0, 127)]
    pltpu.make_async_copy(rest, rest, recv).wait()
    pltpu.make_async_copy(rest, rest, send).wait()


def exchange(x, name):
    return pl.pallas_call(
        exchange_kernel,
        out_shape=jax.ShapeDtypeStruct((128, 16, 128), jnp.float32),
        in_specs=[pl.BlockSpec(memory_space=pltpu.VMEM)],
        out_specs=pl.BlockSpec(memory_space=pltpu.VMEM),
        scratch_shapes=[pltpu.SemaphoreType.DMA, pltpu.SemaphoreType.DMA],
        compiler_params=pltpu.CompilerParams(collective_id=name, has_side_effects=True, vmem_limit_bytes=40 * 2**20),
    )(x)


CHEB = 8


HALF_SPAN = 12.0
TWO_PI = 6.283185307179586


def padded_2(block, sides, width):
    for axis, dim in sides:
        count = lax.axis_size(axis)
        forward = [(i, i + 1) for i in range(count - 1)]
        backward = [(target, source) for source, target in forward]
        low = lax.ppermute(
            lax.slice_in_dim(block, block.shape[dim] - width, None, axis=dim), axis, forward
        )
        high = lax.ppermute(lax.slice_in_dim(block, 0, width, axis=dim), axis, backward)
        block = jnp.concatenate([low, block, high], axis=dim)
    return block


def face_weights(padded):
    core = padded[1:-1, 1:-1, 1:-1]
    return (
        0.5 * (core + padded[2:, 1:-1, 1:-1]),
        0.5 * (core + padded[:-2, 1:-1, 1:-1]),
        0.5 * (core + padded[1:-1, 2:, 1:-1]),
        0.5 * (core + padded[1:-1, :-2, 1:-1]),
        0.5 * (core + padded[1:-1, 1:-1, 2:]),
        0.5 * (core + padded[1:-1, 1:-1, :-2]),
    )


def stiffness(field, faces):
    zpadded = padded_2(field, (("space", 2),), 1)
    padded = jnp.pad(zpadded, ((0, 0), (0, 0), (0, 0), (1, 1), (1, 1)))
    total = faces[0] + faces[1] + faces[2] + faces[3] + faces[4] + faces[5]
    beside = faces[0] * padded[..., 2:, 1:-1, 1:-1] + faces[1] * padded[..., :-2, 1:-1, 1:-1]
    beside = (
        beside + faces[2] * padded[..., 1:-1, 2:, 1:-1] + faces[3] * padded[..., 1:-1, :-2, 1:-1]
    )
    beside = (
        beside + faces[4] * padded[..., 1:-1, 1:-1, 2:] + faces[5] * padded[..., 1:-1, 1:-1, :-2]
    )
    return total * field - beside


def cmul(left, right):
    return (left[0] * right[0] - left[1] * right[1], left[0] * right[1] + left[1] * right[0])


def cinv(value):
    denom = value[0] * value[0] + value[1] * value[1]
    return (value[0] / denom, -value[1] / denom)


def scale_field(factor, field):
    real_f = factor[0][:, None, None, None]
    imag_f = factor[1][:, None, None, None]
    return jnp.stack([real_f * field[0] - imag_f * field[1], real_f * field[1] + imag_f * field[0]])


def angle_table(count, sign):
    index = jnp.arange(count, dtype=jnp.int32)
    product = index[:, None] * index[None, :] % count
    angle = sign * TWO_PI * product.astype(jnp.float32) / count
    return (jnp.cos(angle), jnp.sin(angle))


def body(source, start_field, last_guess, classes, conductivity, alpha_num):
    source = exchange(exchange(source.reshape(128, 16, 128), 1), 1).reshape(source.shape)
    lt_dev = source.shape[0]
    n_tm = lax.axis_size("tm")
    steps = lt_dev * n_tm
    tm_index = lax.axis_index("tm")
    alpha = alpha_num[0].astype(jnp.float32) / 32.0
    log_alpha = jnp.log(alpha)
    slots = jnp.arange(lt_dev, dtype=jnp.int32)
    times = (tm_index * lt_dev + slots).astype(jnp.float32)
    scale = jnp.exp(log_alpha * times / steps)
    first = jnp.where(tm_index == 0, 1.0, 0.0).astype(jnp.float32)
    rhs = source.at[0].add((start_field - alpha * last_guess) * first)
    weighted = rhs * scale[:, None, None, None]
    levels = jnp.arange(conductivity.shape[0], dtype=jnp.int32)
    kappa = jnp.sum(
        jnp.where(
            classes[None] == levels[:, None, None, None], conductivity[:, None, None, None], 0.0
        ),
        axis=0,
    )
    kappa_pad = padded_2(kappa, (("space", 0),), 1)
    faces = face_weights(jnp.pad(kappa_pad, ((0, 0), (1, 1), (1, 1))))
    block = lax.all_to_all(weighted, "tm", split_axis=2, concat_axis=0, tiled=True)
    cos_t, sin_t = angle_table(steps, -1.0)
    real_part = jnp.einsum("kn,ncxy->kcxy", cos_t, block, precision=lax.Precision.HIGHEST)
    imag_part = jnp.einsum("kn,ncxy->kcxy", sin_t, block, precision=lax.Precision.HIGHEST)
    spread = jnp.stack([real_part, imag_part])
    spectrum = lax.all_to_all(spread, "tm", split_axis=1, concat_axis=3, tiled=True)
    freqs = tm_index * lt_dev + slots
    ratio = jnp.exp(log_alpha / steps)
    phase = TWO_PI * (freqs % steps).astype(jnp.float32) / steps
    shift = (1.0 - ratio * jnp.cos(phase), ratio * jnp.sin(phase))
    center = (shift[0] + HALF_SPAN, shift[1])
    sigma = (center[0] / HALF_SPAN, center[1] / HALF_SPAN)
    rho = cinv(sigma)
    direction = scale_field(cinv(center), spectrum)
    solution = direction
    residual = spectrum
    for sweep in range(CHEB):
        image = scale_field(shift, direction) + stiffness(direction, faces)
        residual = residual - image
        rho_next = cinv((2.0 * sigma[0] - rho[0], 2.0 * sigma[1] - rho[1]))
        step_gain = (2.0 * rho_next[0] / HALF_SPAN, 2.0 * rho_next[1] / HALF_SPAN)
        direction = scale_field(cmul(rho_next, rho), direction) + scale_field(step_gain, residual)
        solution = solution + direction
        rho = rho_next
    block = lax.all_to_all(solution, "tm", split_axis=3, concat_axis=1, tiled=True)
    cos_t, sin_t = angle_table(steps, 1.0)
    real_part = jnp.einsum(
        "nk,kcxy->ncxy", cos_t, block[0], precision=lax.Precision.HIGHEST
    ) - jnp.einsum("nk,kcxy->ncxy", sin_t, block[1], precision=lax.Precision.HIGHEST)
    gathered = real_part / steps
    back = lax.all_to_all(gathered, "tm", split_axis=0, concat_axis=2, tiled=True)
    return back * jnp.exp(-log_alpha * times / steps)[:, None, None, None]


def solution(mesh):
    placed = (
        P("tm", "space", None, None),
        P("space", None, None),
        P("space", None, None),
        P("space", None, None),
        P(),
        P(),
    )
    return jax.shard_map(
        body, mesh=mesh, in_specs=placed, out_specs=P("tm", "space", None, None), check_vma=False
    )
```

```python
import functools

import jax
import jax.numpy as jnp
import numpy as np
from jax import lax
from jax.experimental import pallas as pl
from jax.experimental.pallas import tpu as pltpu
from jax.sharding import PartitionSpec as P

MESH = pl.DeviceIdType.MESH
F32 = jnp.float32
CHEB = 8
STEPS = 32
HALF_SPAN = 12.0
NTM, NSP = 16, 8
NDEV = NTM * NSP
LOWX, HIGHX, LOWY, HIGHY = 0, 1, 2, 3


def tables():
    lane = np.arange(128)
    slot, pair = lane // 8, lane % 8
    dft = np.zeros((2, 128, 2, 128))
    back = np.zeros((2, 128, 2, 128))
    same = (pair[:, None] == pair[None, :]).astype(np.float64)
    for half in range(2):
        n = 2 * slot + half
        angle = 2 * np.pi * ((n[:, None] * slot[None, :]) % STEPS) / STEPS
        sign = np.where(n % 2 == 0, 1.0, -1.0)[:, None]
        first = (slot == 0)[None, :]
        real = np.cos(angle)
        imag = np.where(first, sign, -np.sin(angle))
        weight = np.where(first, 1.0, 2.0) / STEPS
        dft[half, :, 0, :] = same * real
        dft[half, :, 1, :] = same * imag
        back[0, :, half, :] = (same * real * weight).T
        back[1, :, half, :] = (same * imag * weight).T
    trig = np.zeros((16, 128))
    for row in range(8):
        freq = np.where((slot == 0) & (row >= 4), 16, slot)
        angle = 2 * np.pi * freq / STEPS
        trig[row] = np.cos(angle)
        trig[8 + row] = np.where(slot == 0, 0.0, np.sin(angle))
    return (
        dft.reshape(256, 256).astype(np.float32),
        back.reshape(256, 256).astype(np.float32),
        trig.astype(np.float32),
    )


def cmul(a, b):
    return (a[0] * b[0] - a[1] * b[1], a[0] * b[1] + a[1] * b[0])


def cinv(a):
    denom = a[0] * a[0] + a[1] * a[1]
    return (a[0] / denom, -a[1] / denom)


def chebyshev_table(log_alpha, cos_f, sin_f):
    ratio = jnp.exp(log_alpha / STEPS)
    center = (1.0 - ratio * cos_f + HALF_SPAN, ratio * sin_f)
    sigma = (center[0] / HALF_SPAN, center[1] / HALF_SPAN)
    rho = [cinv(sigma)]
    for _ in range(CHEB):
        rho.append(cinv((2.0 * sigma[0] - rho[-1][0], 2.0 * sigma[1] - rho[-1][1])))
    inner = (jnp.ones_like(cos_f), jnp.zeros_like(cos_f))
    gains = [None] * (CHEB + 1)
    for j in range(CHEB, -1, -1):
        if j < CHEB:
            step = cmul(cmul(rho[j + 1], rho[j]), inner)
            inner = (1.0 + step[0], step[1])
        scale = cinv(center) if j == 0 else (rho[j][0] / 6.0, rho[j][1] / 6.0)
        gains[j] = cmul(scale, inner)
    level = (jnp.ones_like(cos_f), jnp.zeros_like(cos_f))
    terms = []
    for j in range(CHEB + 1):
        terms.append(cmul(gains[j], level))
        level = cmul(level, rho[j])
    zero = (jnp.zeros_like(cos_f), jnp.zeros_like(cos_f))
    terms += [zero, zero]
    out = []
    for j in range(CHEB + 1):
        own = terms[j] if j == 0 else (0.5 * terms[j][0], 0.5 * terms[j][1])
        out.append((own[0] - 0.5 * terms[j + 2][0], own[1] - 0.5 * terms[j + 2][1]))
    return out


def swap_groups(a):
    group = lax.broadcasted_iota(jnp.int32, a[0].shape, 1) // 32
    upper = group >= 2
    odd = group % 2 == 1
    c0 = jnp.where(upper, pltpu.roll(a[2], 64, 1), a[0])
    c2 = jnp.where(upper, a[2], pltpu.roll(a[0], 64, 1))
    c1 = jnp.where(upper, pltpu.roll(a[3], 64, 1), a[1])
    c3 = jnp.where(upper, a[3], pltpu.roll(a[1], 64, 1))
    return (
        jnp.where(odd, pltpu.roll(c1, 32, 1), c0),
        jnp.where(odd, c1, pltpu.roll(c0, 96, 1)),
        jnp.where(odd, pltpu.roll(c3, 32, 1), c2),
        jnp.where(odd, c3, pltpu.roll(c2, 96, 1)),
    )


def tile_of(tm, sp):
    cx, cz, cy, core = tm // 4, tm % 4, sp // 2, sp % 2
    zhi = cz // 2
    zlo = (cz + 1) // 2 % 2
    a = cx + zlo * (7 - 2 * cx)
    b = cy + zhi * (7 - 2 * cy)
    return 2 * a + core, b


def device_of(xi, yi):
    a, core = xi // 2, xi % 2
    zlo, zhi = a // 4, yi // 4
    cx = a + zlo * (7 - 2 * a)
    cy = yi + zhi * (7 - 2 * yi)
    cz = zlo + zhi * (3 - 2 * zlo)
    return cx * 4 + cz, cy * 2 + core


def dot(a, b):
    return jnp.dot(a, b, precision=lax.Precision.HIGHEST, preferred_element_type=F32)


def kernel(
    anum, cond, source, start, guess, classes, dft, back, trig, out,
    send1, recv1, send2, recv2, cls_send, cls_recv, kap, kys, kyr, wx, wym, wyp, wzi, wzm, wzp, wc,
    u, ys, yr, acc, beta, tsem, ksend, krecv, hsend, hrecv,
):
    tm = lax.axis_index("tm")
    sp = lax.axis_index("space")
    me = tm * NSP + sp
    xi, yi = tile_of(tm, sp)
    tile = xi * 8 + yi

    barrier = pltpu.get_barrier_semaphore()

    zrow = jnp.zeros((2, 2, 32, 128), F32)
    for slot in range(2):
        u[slot, 0] = zrow
        u[slot, 17] = zrow
        for side in range(2):
            yr[slot, side] = jnp.zeros((64, 128), F32)
    kap[0] = jnp.zeros((2, 32, 128), F32)
    kap[17] = jnp.zeros((2, 32, 128), F32)
    for side in range(2):
        kyr[side] = jnp.zeros((32, 128), F32)

    def greet(k, carry):
        t = (me + k) % NDEV
        pl.semaphore_signal(barrier, inc=1, device_id=(t // NSP, t % NSP), device_id_type=MESH)
        return carry

    lax.fori_loop(1, NDEV, greet, 0)

    log_alpha = jnp.log(jnp.full((8, 128), anum[0].astype(F32) / 32.0, F32))
    alpha_row = jnp.full((8, 128), anum[0].astype(F32) / 32.0, F32)
    first = jnp.where(tm == 0, 1.0, 0.0).astype(F32)
    n0 = (2 * tm).astype(F32)
    scales = [jnp.exp(log_alpha * (n0 + t) / STEPS) for t in range(2)]
    unscales = [jnp.exp(-log_alpha * (n0 + t) / STEPS) for t in range(2)]

    zhi = tm % 4 // 2
    half_lanes = pl.ds(pl.multiple_of(zhi * 128, 128), 128)
    for core in range(2):
        xc = (xi // 2) * 2 + core
        parts = [
            classes[z, pl.ds(pl.multiple_of(xc * 16 + xt * 8, 8), 8), half_lanes]
            for xt in range(2)
            for z in range(2)
        ]
        for j, value in enumerate(swap_groups(parts)):
            cls_send[core, j] = value

    def pack(x, carry):
        for xt in range(2):
            rows = pl.ds(pl.multiple_of(x * 16 + xt * 8, 8), 8)
            for h in range(2):
                lanes = slice(h * 128, h * 128 + 128)
                parts = []
                for t in range(2):
                    for z in range(2):
                        value = source[t, z, rows, lanes]
                        if t == 0:
                            value = value + (start[z, rows, lanes] - alpha_row * guess[z, rows, lanes]) * first
                        parts.append(value * scales[t])
                for j, value in enumerate(swap_groups(parts)):
                    at = pl.multiple_of((x * 8 + h * 4 + j) * 16 + xt * 8, 8)
                    send1[pl.ds(at, 8), :] = value
        return carry

    lax.fori_loop(0, 16, pack, 0)

    for j, (re, im) in enumerate(chebyshev_table(log_alpha, trig[0:8, :], trig[8:16, :])):
        beta[j, 0] = re
        beta[j, 1] = im

    pl.semaphore_wait(barrier, NDEV - 1)

    def cls_go(k, carry):
        other = (sp + k) % NSP
        ocy, ocore = other // 2, other % 2
        j = ocy + zhi * (3 - 2 * ocy)
        pltpu.make_async_remote_copy(
            src_ref=cls_send.at[ocore, j],
            dst_ref=cls_recv.at[pl.ds(pl.multiple_of(sp * 8, 8), 8)],
            send_sem=tsem.at[4],
            recv_sem=tsem.at[5],
            device_id=(tm, other),
            device_id_type=MESH,
        ).start()
        return carry

    lax.fori_loop(1, NSP, cls_go, 0)

    def rows16(index):
        return pl.ds(pl.multiple_of(index * 16, 16), 16)

    def t1_go(k, carry):
        kk = (k * 37) % NDEV
        t0 = (tm // 4 + kk // 32) % 4 * 4 + (tm + kk // 8) % 4
        t1 = (sp // 2 + kk // 2) % 4 * 2 + (sp + kk) % 2
        ox, oy = tile_of(t0, t1)
        pltpu.make_async_remote_copy(
            src_ref=send1.at[rows16(ox * 8 + oy)],
            dst_ref=recv1.at[rows16(me)],
            send_sem=tsem.at[0],
            recv_sem=tsem.at[1],
            device_id=(t0, t1),
            device_id_type=MESH,
        ).start()
        return carry

    lax.fori_loop(1, NDEV, t1_go, 0)
    recv1[rows16(me), :] = send1[rows16(tile), :]
    mycy, mycore = sp // 2, sp % 2
    cls_recv[pl.ds(pl.multiple_of(sp * 8, 8), 8), :] = cls_send[mycore, mycy + zhi * (3 - 2 * mycy)]

    some = cls_recv.at[pl.ds(0, 56)]
    pltpu.make_async_copy(some, some, tsem.at[5]).wait()

    def conductivities(xx, carry):
        codes = cls_recv[pl.ds(xx, 8, stride=8), :]
        value = jnp.zeros((8, 128), F32)
        for level in range(8):
            value = jnp.where(codes == level, cond[level], value)
        full = jnp.concatenate([value] * 16, axis=0).T
        for xt in range(2):
            block = full[xt * 64 : xt * 64 + 64].reshape(2, 32, 128)
            kap[1 + xt * 8 + xx] = block
            for z in range(2):
                row = pl.ds((xt * 8 + xx) * 2 + z, 1)
                kys[0, row, :] = block[z, 0:1]
                kys[1, row, :] = block[z, 31:32]
        return carry

    lax.fori_loop(0, 8, conductivities, 0)

    has = [xi > 0, xi < 15, yi > 0, yi < 7]
    near = [
        device_of(jnp.maximum(xi - 1, 0), yi),
        device_of(jnp.minimum(xi + 1, 15), yi),
        device_of(xi, jnp.maximum(yi - 1, 0)),
        device_of(xi, jnp.minimum(yi + 1, 7)),
    ]

    def kap_copy(side):
        src, dst = [
            (kap.at[1], kap.at[17]),
            (kap.at[16], kap.at[0]),
            (kys.at[0], kyr.at[1]),
            (kys.at[1], kyr.at[0]),
        ][side]
        return pltpu.make_async_remote_copy(
            src_ref=src, dst_ref=dst, send_sem=ksend.at[side], recv_sem=krecv.at[side ^ 1],
            device_id=near[side], device_id_type=MESH,
        )

    def kap_wait(side):
        dst = [kap.at[0], kap.at[17], kyr.at[0], kyr.at[1]][side]
        pltpu.make_async_copy(dst, dst, krecv.at[side]).wait()

    def u_copy(slot, side):
        src, dst = [
            (u.at[slot, 1], u.at[slot, 17]),
            (u.at[slot, 16], u.at[slot, 0]),
            (ys.at[slot, 0], yr.at[slot, 1]),
            (ys.at[slot, 1], yr.at[slot, 0]),
        ][side]
        return pltpu.make_async_remote_copy(
            src_ref=src, dst_ref=dst, send_sem=hsend.at[slot, side], recv_sem=hrecv.at[slot, side ^ 1],
            device_id=near[side], device_id_type=MESH,
        )

    def u_wait(slot, side):
        dst = [u.at[slot, 0], u.at[slot, 17], yr.at[slot, 0], yr.at[slot, 1]][side]
        pltpu.make_async_copy(dst, dst, hrecv.at[slot, side]).wait()

    for side in range(4):

        @pl.when(has[side])
        def _(side=side):
            kap_copy(side).start()

    for side in range(4):

        @pl.when(has[side])
        def _(side=side):
            kap_wait(side)

    row_at = lax.broadcasted_iota(jnp.int32, (32, 128), 0)
    pair_at = lax.broadcasted_iota(jnp.int32, (32, 128), 1) % 8

    def weights(x, carry):
        total = [None, None]
        k = [kap[x + 1, z] for z in range(2)]
        for z in range(2):
            row = pl.ds(x * 2 + z, 1)
            low = (k[z] + kap[x, z]) * (1.0 / 12.0)
            high = (k[z] + kap[x + 2, z]) * (1.0 / 12.0)
            wx[x, z] = low

            @pl.when(x == 15)
            def _(z=z, high=high):
                wx[16, z] = high

            before = jnp.where(row_at == 0, kyr[0, row, :], pltpu.roll(k[z], 1, 0))
            after = jnp.where(row_at == 31, kyr[1, row, :], pltpu.roll(k[z], 31, 0))
            before = (k[z] + before) * (1.0 / 12.0)
            after = (k[z] + after) * (1.0 / 12.0)
            wym[x, z] = before
            wyp[x, z] = after
            total[z] = (low + high) + (before + after)
        inside = (k[0] + k[1]) * (1.0 / 12.0)
        below = (k[0] + jnp.where(pair_at == 0, 0.0, pltpu.roll(k[1], 1, 1))) * (1.0 / 12.0)
        above = (k[1] + jnp.where(pair_at == 7, 0.0, pltpu.roll(k[0], 127, 1))) * (1.0 / 12.0)
        wzi[x] = inside
        wzm[x] = jnp.where(pair_at == 0, 0.0, below)
        wzp[x] = jnp.where(pair_at == 7, 0.0, above)
        wc[x, 0] = 2.0 - (total[0] + (inside + below))
        wc[x, 1] = 2.0 - (total[1] + (inside + above))
        return carry

    lax.fori_loop(0, 16, weights, 0)

    most = recv1.at[pl.ds(0, (NDEV - 1) * 16)]
    pltpu.make_async_copy(most, most, tsem.at[1]).wait()

    def put_edges(slot, x, p, z, value):
        row = pl.ds(x * 4 + p * 2 + z, 1)
        ys[slot, 0, row, :] = value[0:1]
        ys[slot, 1, row, :] = value[31:32]

    def forward(x, carry):
        cells = recv1[pl.ds(x, 128, stride=16), :].T
        spectrum = dot(jnp.concatenate([cells[:64], cells[64:]], axis=1), dft[...])
        for p in range(2):
            for z in range(2):
                value = spectrum[z * 32 : z * 32 + 32, p * 128 : p * 128 + 128]
                u[0, x + 1, p, z] = value
                u[1, x + 1, p, z] = jnp.zeros((32, 128), F32)
                put_edges(0, x, p, z, value)
        return carry

    lax.fori_loop(0, 16, forward, 0)

    for j in range(CHEB):
        now, new = j % 2, (j + 1) % 2
        last = j == CHEB - 1
        for side in range(4):

            @pl.when(has[side])
            def _(side=side, now=now):
                u_copy(now, side).start()

        for side in range(4):

            @pl.when(has[side])
            def _(side=side, now=now):
                u_wait(now, side)
                u_copy(now, side).wait_send()

        def sweep(x, carry, j=j, now=now, new=new, last=last):
            got = []
            for p in range(2):
                mid = [u[now, x + 1, p, z] for z in range(2)]
                for z in range(2):
                    row = pl.ds(x * 4 + p * 2 + z, 1)
                    before = jnp.where(row_at == 0, yr[now, 0, row, :], pltpu.roll(mid[z], 1, 0))
                    after = jnp.where(row_at == 31, yr[now, 1, row, :], pltpu.roll(mid[z], 31, 0))
                    total = wc[x, z] * mid[z]
                    total = total + (wx[x, z] * u[now, x, p, z] + wx[x + 1, z] * u[now, x + 2, p, z])
                    total = total + (wym[x, z] * before + wyp[x, z] * after)
                    if z == 0:
                        total = total + (wzi[x] * mid[1] + wzm[x] * pltpu.roll(mid[1], 1, 1))
                    else:
                        total = total + (wzi[x] * mid[0] + wzp[x] * pltpu.roll(mid[0], 127, 1))
                    prev = u[new, x + 1, p, z]
                    value = total - prev
                    if not last:
                        u[new, x + 1, p, z] = value
                        put_edges(new, x, p, z, value)
                    got.append((prev, mid[z], value))
            if j % 3 == 1:
                for z in range(2):
                    real, imag = None, None
                    for i in range(3):
                        a, b = got[z][i], got[2 + z][i]
                        br0, br1 = beta[j - 1 + i, 0, 0:1, :], beta[j - 1 + i, 0, 4:5, :]
                        bi = beta[j - 1 + i, 1, 0:1, :]
                        re = br0 * a - bi * b
                        im = br1 * b + bi * a
                        real = re if real is None else real + re
                        imag = im if imag is None else imag + im
                    if j > 1:
                        real = real + acc[x, 0, z]
                        imag = imag + acc[x, 1, z]
                    acc[x, 0, z] = real
                    acc[x, 1, z] = imag
            return carry

        lax.fori_loop(0, 16, sweep, 0)

    def inverse(x, carry):
        both = jnp.concatenate([acc[x, 0].reshape(64, 128), acc[x, 1].reshape(64, 128)], axis=1)
        times = dot(both, back[...])
        cells = jnp.concatenate([times[:, :128], times[:, 128:]], axis=0)
        send2[pl.ds(x, 128, stride=16), :] = cells.T
        return carry

    lax.fori_loop(0, 16, inverse, 0)

    def t2_go(k, carry):
        kk = (k * 37) % NDEV
        t0 = (tm // 4 + kk // 32) % 4 * 4 + (tm + kk // 8) % 4
        t1 = (sp // 2 + kk // 2) % 4 * 2 + (sp + kk) % 2
        pltpu.make_async_remote_copy(
            src_ref=send2.at[rows16(t0 * NSP + t1)],
            dst_ref=recv2.at[rows16(tile)],
            send_sem=tsem.at[2],
            recv_sem=tsem.at[3],
            device_id=(t0, t1),
            device_id_type=MESH,
        ).start()
        return carry

    lax.fori_loop(1, NDEV, t2_go, 0)
    recv2[rows16(tile), :] = send2[rows16(me), :]
    most2 = recv2.at[pl.ds(0, (NDEV - 1) * 16)]
    pltpu.make_async_copy(most2, most2, tsem.at[3]).wait()

    def unpack(x, carry):
        for xt in range(2):
            rows = pl.ds(pl.multiple_of(x * 16 + xt * 8, 8), 8)
            for h in range(2):
                parts = [
                    recv2[pl.ds(pl.multiple_of((x * 8 + h * 4 + j) * 16 + xt * 8, 8), 8), :]
                    for j in range(4)
                ]
                for i, value in enumerate(swap_groups(parts)):
                    out[i // 2, i % 2, rows, h * 128 : h * 128 + 128] = value * unscales[i // 2]
        return carry

    lax.fori_loop(0, 16, unpack, 0)

    pltpu.make_async_copy(most, most, tsem.at[0]).wait()
    pltpu.make_async_copy(most2, most2, tsem.at[2]).wait()
    pltpu.make_async_copy(some, some, tsem.at[4]).wait()
    for side in range(4):

        @pl.when(has[side])
        def _(side=side):
            kap_copy(side).wait_send()


def body(source, start_field, last_guess, classes, conductivity, alpha_num):
    dft, back, trig = (jnp.asarray(t) for t in tables())
    smem = pl.BlockSpec(memory_space=pltpu.SMEM)
    vmem = pl.BlockSpec(memory_space=pltpu.VMEM)
    V = pltpu.VMEM
    return pl.pallas_call(
        kernel,
        out_shape=jax.ShapeDtypeStruct((2, 2, 256, 256), F32),
        in_specs=[smem, smem] + [vmem] * 7,
        out_specs=vmem,
        scratch_shapes=[
            V((2048, 128), F32), V((2048, 128), F32), V((2048, 128), F32), V((2048, 128), F32),
            V((2, 4, 8, 128), jnp.int32), V((64, 128), jnp.int32),
            V((18, 2, 32, 128), F32), V((2, 32, 128), F32), V((2, 32, 128), F32),
            V((17, 2, 32, 128), F32), V((16, 2, 32, 128), F32), V((16, 2, 32, 128), F32),
            V((16, 32, 128), F32), V((16, 32, 128), F32), V((16, 32, 128), F32), V((16, 2, 32, 128), F32),
            V((2, 18, 2, 2, 32, 128), F32), V((2, 2, 64, 128), F32), V((2, 2, 64, 128), F32),
            V((16, 2, 2, 32, 128), F32), V((CHEB + 1, 2, 8, 128), F32),
            pltpu.SemaphoreType.DMA((6,)),
            pltpu.SemaphoreType.DMA((4,)), pltpu.SemaphoreType.DMA((4,)),
            pltpu.SemaphoreType.DMA((2, 4)), pltpu.SemaphoreType.DMA((2, 4)),
        ],
        compiler_params=pltpu.CompilerParams(
            collective_id=1, has_side_effects=True, vmem_limit_bytes=48 * 2**20
        ),
    )(alpha_num, conductivity, source, start_field, last_guess, classes, dft, back, trig)


def solution(mesh):
    placed = (
        P("tm", "space", None, None),
        P("space", None, None),
        P("space", None, None),
        P("space", None, None),
        P(),
        P(),
    )
    return jax.shard_map(
        body, mesh=mesh, in_specs=placed, out_specs=P("tm", "space", None, None), check_vma=False
    )
```

```python
import functools

import jax
import jax.numpy as jnp
import numpy as np
from jax import lax
from jax.experimental import pallas as pl
from jax.experimental.pallas import tpu as pltpu
from jax.sharding import PartitionSpec as P

MESH = pl.DeviceIdType.MESH
F32 = jnp.float32
CHEB = 8
STEPS = 32
HALF_SPAN = 12.0
NTM, NSP = 16, 8
NDEV = NTM * NSP
DEPTH = 4
BLOCK = 4
UNROLL = 2
SIDES = [(dx, dy) for dx in (-1, 0, 1) for dy in (-1, 0, 1) if (dx, dy) != (0, 0)]


def tables():
    lane = np.arange(128)
    slot, pair = lane // 8, lane % 8
    dft = np.zeros((2, 128, 2, 128))
    back = np.zeros((2, 128, 2, 128))
    same = (pair[:, None] == pair[None, :]).astype(np.float64)
    for half in range(2):
        n = 2 * slot + half
        angle = 2 * np.pi * ((n[:, None] * slot[None, :]) % STEPS) / STEPS
        sign = np.where(n % 2 == 0, 1.0, -1.0)[:, None]
        first = (slot == 0)[None, :]
        real = np.cos(angle)
        imag = np.where(first, sign, -np.sin(angle))
        weight = np.where(first, 1.0, 2.0) / STEPS
        dft[half, :, 0, :] = same * real
        dft[half, :, 1, :] = same * imag
        back[0, :, half, :] = (same * real * weight).T
        back[1, :, half, :] = (same * imag * weight).T
    trig = np.zeros((16, 128))
    for row in range(8):
        freq = np.where((slot == 0) & (row >= 4), 16, slot)
        angle = 2 * np.pi * freq / STEPS
        trig[row] = np.cos(angle)
        trig[8 + row] = np.where(slot == 0, 0.0, np.sin(angle))
    return (
        dft.reshape(256, 256).astype(np.float32),
        back.reshape(256, 256).astype(np.float32),
        trig.astype(np.float32),
    )


def cmul(a, b):
    return (a[0] * b[0] - a[1] * b[1], a[0] * b[1] + a[1] * b[0])


def cinv(a):
    denom = a[0] * a[0] + a[1] * a[1]
    return (a[0] / denom, -a[1] / denom)


def chebyshev_table(log_alpha, cos_f, sin_f):
    ratio = jnp.exp(log_alpha / STEPS)
    center = (1.0 - ratio * cos_f + HALF_SPAN, ratio * sin_f)
    sigma = (center[0] / HALF_SPAN, center[1] / HALF_SPAN)
    rho = [cinv(sigma)]
    for _ in range(CHEB):
        rho.append(cinv((2.0 * sigma[0] - rho[-1][0], 2.0 * sigma[1] - rho[-1][1])))
    inner = (jnp.ones_like(cos_f), jnp.zeros_like(cos_f))
    gains = [None] * (CHEB + 1)
    for j in range(CHEB, -1, -1):
        if j < CHEB:
            step = cmul(cmul(rho[j + 1], rho[j]), inner)
            inner = (1.0 + step[0], step[1])
        scale = cinv(center) if j == 0 else (rho[j][0] / 6.0, rho[j][1] / 6.0)
        gains[j] = cmul(scale, inner)
    level = (jnp.ones_like(cos_f), jnp.zeros_like(cos_f))
    terms = []
    for j in range(CHEB + 1):
        terms.append(cmul(gains[j], level))
        level = cmul(level, rho[j])
    zero = (jnp.zeros_like(cos_f), jnp.zeros_like(cos_f))
    terms += [zero, zero]
    out = []
    for j in range(CHEB + 1):
        own = terms[j] if j == 0 else (0.5 * terms[j][0], 0.5 * terms[j][1])
        out.append((own[0] - 0.5 * terms[j + 2][0], own[1] - 0.5 * terms[j + 2][1]))
    for m in range(BLOCK, 0, -1):
        for j in range(BLOCK + m - 2, BLOCK - m - 1, -2):
            out[j] = (out[j][0] - out[BLOCK + m][0], out[j][1] - out[BLOCK + m][1])
    return out


def swap_groups(a):
    group = lax.broadcasted_iota(jnp.int32, a[0].shape, 1) // 32
    upper = group >= 2
    odd = group % 2 == 1
    c0 = jnp.where(upper, pltpu.roll(a[2], 64, 1), a[0])
    c2 = jnp.where(upper, a[2], pltpu.roll(a[0], 64, 1))
    c1 = jnp.where(upper, pltpu.roll(a[3], 64, 1), a[1])
    c3 = jnp.where(upper, a[3], pltpu.roll(a[1], 64, 1))
    return (
        jnp.where(odd, pltpu.roll(c1, 32, 1), c0),
        jnp.where(odd, c1, pltpu.roll(c0, 96, 1)),
        jnp.where(odd, pltpu.roll(c3, 32, 1), c2),
        jnp.where(odd, c3, pltpu.roll(c2, 96, 1)),
    )


def tile_of(tm, sp):
    cx, cz, cy, core = tm // 4, tm % 4, sp // 2, sp % 2
    zhi = cz // 2
    zlo = (cz + 1) // 2 % 2
    a = cx + zlo * (7 - 2 * cx)
    b = cy + zhi * (7 - 2 * cy)
    return 2 * a + core, b


def device_of(xi, yi):
    a, core = xi // 2, xi % 2
    zlo, zhi = a // 4, yi // 4
    cx = a + zlo * (7 - 2 * a)
    cy = yi + zhi * (7 - 2 * yi)
    cz = zlo + zhi * (3 - 2 * zlo)
    return cx * 4 + cz, cy * 2 + core


def two_terms(a):
    head = a.astype(jnp.bfloat16)
    return head, (a - head.astype(F32)).astype(jnp.bfloat16)


def dot(a, head, rest):
    a_head, a_rest = two_terms(a)
    small = jnp.dot(a_rest, head, preferred_element_type=F32) + jnp.dot(a_head, rest, preferred_element_type=F32)
    return jnp.dot(a_head, head, preferred_element_type=F32) + small


def kernel(
    anum, cond, source_in, start_in, guess_in, classes_in, dft_in, back_in, trig_in, out,
    source, start, guess, classes, dft, back, dft0, dft1, back0, back1, trig, insem, send1, recv1, send2, recv2, cls_send, cls_recv, kap, wxm, wxp, wym, wyp, wzi, wzm, wzp, wc,
    u0, u1, u2, u3, acc, beta, tsem, ksend, krecv, hsend, hrecv, outsem,
):
    tm = lax.axis_index("tm")
    sp = lax.axis_index("space")
    me = tm * NSP + sp
    xi, yi = tile_of(tm, sp)
    tile = xi * 8 + yi

    zhi = tm % 4 // 2
    half_lanes = pl.ds(pl.multiple_of(zhi * 128, 128), 128)
    pair_rows = pl.ds(pl.multiple_of(xi // 2 * 32, 32), 32)
    pairs = [
        (source_in, source),
        (classes_in.at[:, pair_rows, half_lanes], classes),
        (trig_in, trig),
        (dft_in, dft),
        (back_in, back),
    ]
    loads = [pltpu.make_async_copy(a, b, insem.at[i]) for i, (a, b) in enumerate(pairs)]
    firsts = [
        pltpu.make_async_copy(start_in, start, insem.at[5]),
        pltpu.make_async_copy(guess_in, guess, insem.at[6]),
    ]
    for copy in loads:
        copy.start()

    @pl.when(tm == 0)
    def _():
        for copy in firsts:
            copy.start()

    barrier = pltpu.get_barrier_semaphore()

    def clear(x, carry):
        kap[x] = jnp.zeros((2, 40, 128), F32)
        for p in range(2):
            u0[p, x] = jnp.zeros((2, 40, 128), F32)
            u3[p, x] = jnp.zeros((2, 40, 128), F32)
        return carry

    lax.fori_loop(0, 24, clear, 0)

    def greet(k, carry):
        t = (me + k) % NDEV
        pl.semaphore_signal(barrier, inc=1, device_id=(t // NSP, t % NSP), device_id_type=MESH)
        return carry

    lax.fori_loop(1, NDEV, greet, 0)

    log_alpha = jnp.log(jnp.full((8, 128), anum[0].astype(F32) / 32.0, F32))
    alpha = anum[0].astype(F32) / 32.0
    n0 = (2 * tm).astype(F32)
    scales = [jnp.exp(log_alpha * (n0 + t) / STEPS) for t in range(2)]
    unscales = [jnp.exp(-log_alpha * (n0 + t) / STEPS) for t in range(2)]

    loads[1].wait()
    for core in range(2):
        parts = [
            classes[z, core * 16 + xt * 8 : core * 16 + xt * 8 + 8, :]
            for xt in range(2)
            for z in range(2)
        ]
        for j, value in enumerate(swap_groups(parts)):
            cls_send[core, j] = value

    loads[0].wait()

    @pl.when(tm == 0)
    def _():
        for copy in firsts:
            copy.wait()

        def correct(x, carry):
            rows = pl.ds(pl.multiple_of(x * 16, 16), 16)
            for z in range(2):
                source[0, z, rows, :] = source[0, z, rows, :] + (start[z, rows, :] - alpha * guess[z, rows, :])
            return carry

        lax.fori_loop(0, 16, correct, 0)

    def pack(x, carry):
        for xt in range(2):
            rows = pl.ds(pl.multiple_of(x * 16 + xt * 8, 8), 8)
            for h in range(2):
                lanes = slice(h * 128, h * 128 + 128)
                parts = []
                for t in range(2):
                    for z in range(2):
                        value = source[t, z, rows, lanes]
                        parts.append(value * scales[t])
                for j, value in enumerate(swap_groups(parts)):
                    at = pl.multiple_of((x * 8 + h * 4 + j) * 16 + xt * 8, 8)
                    send1[pl.ds(at, 8), :] = value
        return carry

    lax.fori_loop(0, 16, pack, 0)

    for copy in loads[2:]:
        copy.wait()
    dft0[...], dft1[...] = two_terms(dft[...])
    back0[...], back1[...] = two_terms(back[...])
    for j, (re, im) in enumerate(chebyshev_table(log_alpha, trig[0:8, :], trig[8:16, :])):
        beta[j, 0:1, :] = re[0:1]
        beta[j, 1:2, :] = im[0:1]
        beta[j, 2:3, :] = -im[0:1]
        beta[j, 3:4, :] = re[4:5]

    pl.semaphore_wait(barrier, NDEV - 1)

    def cls_go(k, carry):
        other = (sp + k) % NSP
        ocy, ocore = other // 2, other % 2
        j = ocy + zhi * (3 - 2 * ocy)
        pltpu.make_async_remote_copy(
            src_ref=cls_send.at[ocore, j],
            dst_ref=cls_recv.at[pl.ds(pl.multiple_of(sp * 8, 8), 8)],
            send_sem=tsem.at[4],
            recv_sem=tsem.at[5],
            device_id=(tm, other),
            device_id_type=MESH,
        ).start()
        return carry

    lax.fori_loop(1, NSP, cls_go, 0)

    def rows16(index):
        return pl.ds(pl.multiple_of(index * 16, 16), 16)

    def t1_go(k, carry):
        kk = (k * 37) % NDEV
        t0 = (tm // 4 + kk // 32) % 4 * 4 + (tm + kk // 8) % 4
        t1 = (sp // 2 + kk // 2) % 4 * 2 + (sp + kk) % 2
        ox, oy = tile_of(t0, t1)
        pltpu.make_async_remote_copy(
            src_ref=send1.at[rows16(ox * 8 + oy)],
            dst_ref=recv1.at[rows16(me)],
            send_sem=tsem.at[0],
            recv_sem=tsem.at[1],
            device_id=(t0, t1),
            device_id_type=MESH,
        ).start()
        return carry

    lax.fori_loop(1, NDEV, t1_go, 0)
    recv1[rows16(me), :] = send1[rows16(tile), :]
    mycy, mycore = sp // 2, sp % 2
    cls_recv[pl.ds(pl.multiple_of(sp * 8, 8), 8), :] = cls_send[mycore, mycy + zhi * (3 - 2 * mycy)]

    some = cls_recv.at[pl.ds(0, 56)]
    pltpu.make_async_copy(some, some, tsem.at[5]).wait()

    def conductivities(xx, carry):
        codes = cls_recv[pl.ds(xx, 8, stride=8), :]
        value = jnp.zeros((8, 128), F32)
        for level in range(8):
            value = jnp.where(codes == level, cond[level], value)
        full = jnp.concatenate([value] * 16, axis=0).T
        for xt in range(2):
            kap[DEPTH + xt * 8 + xx, :, 0:32, :] = full[xt * 64 : xt * 64 + 64].reshape(2, 32, 128)
        return carry

    lax.fori_loop(0, 8, conductivities, 0)

    low_x, high_x, low_y, high_y = xi > 0, xi < 15, yi > 0, yi < 7
    beside = {-1: low_x, 1: high_x}, {-1: low_y, 1: high_y}

    def here(dx, dy):
        if dx and dy:
            return jnp.logical_and(beside[0][dx], beside[1][dy])
        return beside[0][dx] if dx else beside[1][dy]

    def span(d, low, middle, high):
        return {-1: low, 0: middle, 1: high}[d]

    def halo(dx, dy):
        return (
            span(dx, pl.ds(0, DEPTH), pl.ds(DEPTH, 16), pl.ds(DEPTH + 16, DEPTH)),
            span(dy, pl.ds(36, 4), pl.ds(0, 32), pl.ds(32, 4)),
        )

    def edge(dx, dy):
        return (
            span(dx, pl.ds(DEPTH, DEPTH), pl.ds(DEPTH, 16), pl.ds(16, DEPTH)),
            span(dy, pl.ds(0, 4), pl.ds(0, 32), pl.ds(28, 4)),
        )

    def exchange(ref, send, recv, act):
        for i, (dx, dy) in enumerate(SIDES):

            @pl.when(here(dx, dy))
            def _(i=i, dx=dx, dy=dy):
                xs, ys = edge(dx, dy)
                xd, yd = halo(-dx, -dy)
                back_at = SIDES.index((-dx, -dy))
                copy = pltpu.make_async_remote_copy(
                    src_ref=ref.at[xs, :, ys, :],
                    dst_ref=ref.at[xd, :, yd, :],
                    send_sem=send.at[i],
                    recv_sem=recv.at[back_at],
                    device_id=device_of(
                        jnp.clip(xi + dx, 0, 15) if dx else xi, jnp.clip(yi + dy, 0, 7) if dy else yi
                    ),
                    device_id_type=MESH,
                )
                if act == "start":
                    copy.start()
                else:
                    copy.wait_send()
                    xh, yh = halo(dx, dy)
                    got = ref.at[xh, :, yh, :]
                    pltpu.make_async_copy(got, got, recv.at[i]).wait()

    exchange(kap, ksend, krecv, "start")
    exchange(kap, ksend, krecv, "wait")

    row_at = lax.broadcasted_iota(jnp.int32, (40, 128), 0)
    pair_at = lax.broadcasted_iota(jnp.int32, (40, 128), 1) % 8
    one = jnp.ones((40, 128), F32)
    inside_low = jnp.where(low_y, 1.0, 0.0).astype(F32)
    inside_high = jnp.where(high_y, 1.0, 0.0).astype(F32)
    columns = jnp.where(row_at < 32, one, jnp.where(row_at < 36, one * inside_high, one * inside_low)) * (1.0 / 12.0)

    def weights(x, carry):
        total = [None, None]
        inside_x = jnp.logical_and(jnp.logical_or(x >= DEPTH, low_x), jnp.logical_or(x < DEPTH + 16, high_x))
        part = columns * jnp.where(inside_x, 1.0, 0.0).astype(F32)
        k = [kap[x, z] for z in range(2)]
        for z in range(2):
            low = (k[z] + kap[x - 1, z]) * part
            high = (k[z] + kap[x + 1, z]) * part
            wxm[x, z] = low
            wxp[x, z] = high
            before = (k[z] + pltpu.roll(k[z], 1, 0)) * part
            after = (k[z] + pltpu.roll(k[z], 39, 0)) * part
            wym[x, z] = before
            wyp[x, z] = after
            total[z] = (low + high) + (before + after)
        inside = (k[0] + k[1]) * part
        below = (k[0] + jnp.where(pair_at == 0, 0.0, pltpu.roll(k[1], 1, 1))) * part
        above = (k[1] + jnp.where(pair_at == 7, 0.0, pltpu.roll(k[0], 127, 1))) * part
        wzi[x] = inside
        wzm[x] = jnp.where(pair_at == 0, 0.0, below)
        wzp[x] = jnp.where(pair_at == 7, 0.0, above)
        wc[x, 0] = part * 24.0 - (total[0] + (inside + below))
        wc[x, 1] = part * 24.0 - (total[1] + (inside + above))
        return carry

    lax.fori_loop(1, 23, weights, 0)

    most = recv1.at[pl.ds(0, (NDEV - 1) * 16)]
    pltpu.make_async_copy(most, most, tsem.at[1]).wait()

    def forward(quad, carry):
        rows = []
        for i in range(4):
            cells = recv1[pl.ds(quad * 4 + i, 128, stride=16), :].T
            rows.append(jnp.concatenate([cells[:64], cells[64:]], axis=1))
        spectrum = dot(jnp.concatenate(rows, axis=0), dft0[...], dft1[...])
        for i in range(4):
            x = quad * 4 + i
            for z in range(2):
                at = i * 64 + z * 32
                re = spectrum[at : at + 32, 0:128]
                im = spectrum[at : at + 32, 128:256]
                u0[0, DEPTH + x, z, 0:32] = re
                u0[1, DEPTH + x, z, 0:32] = im
                acc[0, x, z] = beta[0, 0:1, :] * re + beta[0, 2:3, :] * im
                acc[1, x, z] = beta[0, 1:2, :] * re + beta[0, 3:4, :] * im
        return carry

    lax.fori_loop(0, 4, forward, 0)

    def swap(block, p, act):
        exchange((u0, u3)[block].at[p], hsend.at[block, p], hrecv.at[block, p], act)

    def chebyshev(block, p):
        begin = (u0, u3)[block]
        for m in range(BLOCK):
            now = (begin, u1, begin, u2)[m]
            old = (None, begin, u1, begin)[m]
            new = (u1, begin, u2, u3)[m]
            last = m == BLOCK - 1
            spare = BLOCK - 1 - m
            h = slice(0, 32 if last else 40)

            def sweep(step, carry, now=now, old=old, new=new, last=last, spare=spare, h=h):
                first = DEPTH - spare + step * UNROLL
                field = [[now[p, first + i, z] for z in range(2)] for i in range(-1, UNROLL + 1)]
                values = []
                for i in range(UNROLL):
                    x = first + i
                    below, mid, above = field[i], field[i + 1], field[i + 2]
                    for z in range(2):
                        other = mid[1 - z][h]
                        outer = pltpu.roll(other, 1 if z == 0 else 127, 1)
                        before = pltpu.roll(mid[z], 1, 0)[h]
                        after = pltpu.roll(mid[z], 39, 0)[h]
                        value = wc[x, z, h] * mid[z][h] + wzi[x, h] * other
                        value = value + (wxm[x, z, h] * below[z][h] + wxp[x, z, h] * above[z][h])
                        if old is not None:
                            value = value - old[p, x, z, h]
                        rest = wym[x, z, h] * before + wyp[x, z, h] * after
                        value = value + (rest + (wzm if z == 0 else wzp)[x, h] * outer)
                        values.append((x, z, mid[z][h], value))
                if last:
                    totals = []
                    for x, z, own, value in values:
                        terms = [u1[p, x, z, h], old[p, x, z, h], own, value]
                        for to in range(2):
                            at = 2 * p + to
                            total = beta[BLOCK * block + 1, at : at + 1, :] * terms[0]
                            for i in range(1, 4):
                                total = total + beta[BLOCK * block + 1 + i, at : at + 1, :] * terms[i]
                            totals.append((to, x, z, acc[to, x - DEPTH, z] + total))
                    for to, x, z, total in totals:
                        acc[to, x - DEPTH, z] = total
                if not last or block == 0:
                    for x, z, own, value in values:
                        new[p, x, z, h] = value
                return carry

            lax.fori_loop(0, (16 + 2 * spare) // UNROLL, sweep, 0)

    swap(0, 0, "start")
    swap(0, 1, "start")
    for block in range(2):
        for p in range(2):
            swap(block, p, "wait")
            chebyshev(block, p)
            if block == 0:
                swap(1, p, "start")

    def inverse(quad, carry):
        rows = []
        for i in range(4):
            x = quad * 4 + i
            rows.append(
                jnp.concatenate([acc[0, x].reshape(64, 128), acc[1, x].reshape(64, 128)], axis=1)
            )
        times = dot(jnp.concatenate(rows, axis=0), back0[...], back1[...])
        for i in range(4):
            own = times[i * 64 : i * 64 + 64]
            cells = jnp.concatenate([own[:, :128], own[:, 128:]], axis=0)
            send2[pl.ds(quad * 4 + i, 128, stride=16), :] = cells.T
        return carry

    lax.fori_loop(0, 4, inverse, 0)

    def t2_go(k, carry):
        kk = (k * 37) % NDEV
        t0 = (tm // 4 + kk // 32) % 4 * 4 + (tm + kk // 8) % 4
        t1 = (sp // 2 + kk // 2) % 4 * 2 + (sp + kk) % 2
        pltpu.make_async_remote_copy(
            src_ref=send2.at[rows16(t0 * NSP + t1)],
            dst_ref=recv2.at[rows16(tile)],
            send_sem=tsem.at[2],
            recv_sem=tsem.at[3],
            device_id=(t0, t1),
            device_id_type=MESH,
        ).start()
        return carry

    lax.fori_loop(1, NDEV, t2_go, 0)
    recv2[rows16(tile), :] = send2[rows16(me), :]
    most2 = recv2.at[pl.ds(0, (NDEV - 1) * 16)]
    pltpu.make_async_copy(most2, most2, tsem.at[3]).wait()

    def unpack(x, carry):
        for xt in range(2):
            rows = pl.ds(pl.multiple_of(x * 16 + xt * 8, 8), 8)
            for h in range(2):
                parts = [
                    recv2[pl.ds(pl.multiple_of((x * 8 + h * 4 + j) * 16 + xt * 8, 8), 8), :]
                    for j in range(4)
                ]
                for i, value in enumerate(swap_groups(parts)):
                    source[i // 2, i % 2, rows, h * 128 : h * 128 + 128] = value * unscales[i // 2]
        rows = pl.ds(pl.multiple_of(x * 16, 16), 16)
        pltpu.make_async_copy(source.at[:, :, rows, :], out.at[:, :, rows, :], outsem).start()
        return carry

    lax.fori_loop(0, 16, unpack, 0)

    pltpu.make_async_copy(most, most, tsem.at[0]).wait()
    pltpu.make_async_copy(most2, most2, tsem.at[2]).wait()
    pltpu.make_async_copy(some, some, tsem.at[4]).wait()
    pltpu.make_async_copy(source, out, outsem).wait()


def body(source, start_field, last_guess, classes, conductivity, alpha_num):
    consts = [jnp.asarray(t) for t in tables()]
    smem = pl.BlockSpec(memory_space=pltpu.SMEM)
    hbm = pl.BlockSpec(memory_space=pltpu.HBM)
    BF16 = jnp.bfloat16
    V = pltpu.VMEM
    return pl.pallas_call(
        kernel,
        out_shape=jax.ShapeDtypeStruct((2, 2, 256, 256), F32),
        in_specs=[smem, smem] + [hbm] * 7,
        out_specs=hbm,
        scratch_shapes=[
            V((2, 2, 256, 256), F32), V((2, 256, 256), F32), V((2, 256, 256), F32), V((2, 32, 128), jnp.int32),
            V((256, 256), F32), V((256, 256), F32), V((256, 256), BF16), V((256, 256), BF16), V((256, 256), BF16), V((256, 256), BF16), V((16, 128), F32),
            pltpu.SemaphoreType.DMA((7,)),
            V((2048, 128), F32), V((2048, 128), F32), V((2048, 128), F32), V((2048, 128), F32),
            V((2, 4, 8, 128), jnp.int32), V((64, 128), jnp.int32),
            V((24, 2, 40, 128), F32), V((24, 2, 40, 128), F32), V((24, 2, 40, 128), F32), V((24, 2, 40, 128), F32),
            V((24, 2, 40, 128), F32),
            V((24, 40, 128), F32), V((24, 40, 128), F32), V((24, 40, 128), F32), V((24, 2, 40, 128), F32),
            V((2, 24, 2, 40, 128), F32), V((2, 24, 2, 40, 128), F32), V((2, 24, 2, 40, 128), F32), V((2, 24, 2, 40, 128), F32), V((2, 16, 2, 32, 128), F32), V((CHEB + 1, 8, 128), F32),
            pltpu.SemaphoreType.DMA((6,)),
            pltpu.SemaphoreType.DMA((8,)), pltpu.SemaphoreType.DMA((8,)),
            pltpu.SemaphoreType.DMA((2, 2, 8)), pltpu.SemaphoreType.DMA((2, 2, 8)), pltpu.SemaphoreType.DMA,
        ],
        compiler_params=pltpu.CompilerParams(
            collective_id=1, has_side_effects=True, vmem_limit_bytes=62 * 2**20
        ),
    )(alpha_num, conductivity, source, start_field, last_guess, classes, *consts)


def solution(mesh):
    placed = (
        P("tm", "space", None, None),
        P("space", None, None),
        P("space", None, None),
        P("space", None, None),
        P(),
        P(),
    )
    return jax.shard_map(
        body, mesh=mesh, in_specs=placed, out_specs=P("tm", "space", None, None), check_vma=False
    )
```

```python
import functools

import jax
import jax.numpy as jnp
import numpy as np
from jax import lax
from jax.experimental import pallas as pl
from jax.experimental.pallas import tpu as pltpu
from jax.sharding import PartitionSpec as P

MESH = pl.DeviceIdType.MESH
F32 = jnp.float32
CHEB = 8
STEPS = 32
HALF_SPAN = 12.0
NTM, NSP = 16, 8
NDEV = NTM * NSP
OFFSETS = sorted(
    [(dx, dz, dy, dc) for dx in range(4) for dz in range(4) for dy in range(4) for dc in range(2)][1:],
    key=lambda o: -sum(min(d, 4 - d) for d in o[:3]),
)
DEPTH = 4
BLOCK = 4
UNROLL = 2
SIDES = [(dx, dy) for dx in (-1, 0, 1) for dy in (-1, 0, 1) if (dx, dy) != (0, 0)]


def tables():
    lane = np.arange(128)
    slot, pair = lane // 8, lane % 8
    dft = np.zeros((2, 128, 2, 128))
    back = np.zeros((2, 128, 2, 128))
    same = (pair[:, None] == pair[None, :]).astype(np.float64)
    for half in range(2):
        n = 2 * slot + half
        angle = 2 * np.pi * ((n[:, None] * slot[None, :]) % STEPS) / STEPS
        sign = np.where(n % 2 == 0, 1.0, -1.0)[:, None]
        first = (slot == 0)[None, :]
        real = np.cos(angle)
        imag = np.where(first, sign, -np.sin(angle))
        weight = np.where(first, 1.0, 2.0) / STEPS
        dft[half, :, 0, :] = same * real
        dft[half, :, 1, :] = same * imag
        back[0, :, half, :] = (same * real * weight).T
        back[1, :, half, :] = (same * imag * weight).T
    trig = np.zeros((16, 128))
    for row in range(8):
        freq = np.where((slot == 0) & (row >= 4), 16, slot)
        angle = 2 * np.pi * freq / STEPS
        trig[row] = np.cos(angle)
        trig[8 + row] = np.where(slot == 0, 0.0, np.sin(angle))
    return (
        dft.reshape(256, 256).astype(np.float32),
        back.reshape(256, 256).astype(np.float32),
        trig.astype(np.float32),
    )


def cmul(a, b):
    return (a[0] * b[0] - a[1] * b[1], a[0] * b[1] + a[1] * b[0])


def cinv(a):
    denom = a[0] * a[0] + a[1] * a[1]
    return (a[0] / denom, -a[1] / denom)


def chebyshev_table(log_alpha, cos_f, sin_f):
    ratio = jnp.exp(log_alpha / STEPS)
    center = (1.0 - ratio * cos_f + HALF_SPAN, ratio * sin_f)
    sigma = (center[0] / HALF_SPAN, center[1] / HALF_SPAN)
    rho = [cinv(sigma)]
    for _ in range(CHEB):
        rho.append(cinv((2.0 * sigma[0] - rho[-1][0], 2.0 * sigma[1] - rho[-1][1])))
    inner = (jnp.ones_like(cos_f), jnp.zeros_like(cos_f))
    gains = [None] * (CHEB + 1)
    for j in range(CHEB, -1, -1):
        if j < CHEB:
            step = cmul(cmul(rho[j + 1], rho[j]), inner)
            inner = (1.0 + step[0], step[1])
        scale = cinv(center) if j == 0 else (rho[j][0] / 6.0, rho[j][1] / 6.0)
        gains[j] = cmul(scale, inner)
    level = (jnp.ones_like(cos_f), jnp.zeros_like(cos_f))
    terms = []
    for j in range(CHEB + 1):
        terms.append(cmul(gains[j], level))
        level = cmul(level, rho[j])
    zero = (jnp.zeros_like(cos_f), jnp.zeros_like(cos_f))
    terms += [zero, zero]
    out = []
    for j in range(CHEB + 1):
        own = terms[j] if j == 0 else (0.5 * terms[j][0], 0.5 * terms[j][1])
        out.append((own[0] - 0.5 * terms[j + 2][0], own[1] - 0.5 * terms[j + 2][1]))
    for m in range(BLOCK, 0, -1):
        for j in range(BLOCK + m - 2, BLOCK - m - 1, -2):
            out[j] = (out[j][0] - out[BLOCK + m][0], out[j][1] - out[BLOCK + m][1])
    return out


def swap_groups(a):
    group = lax.broadcasted_iota(jnp.int32, a[0].shape, 1) // 32
    upper = group >= 2
    odd = group % 2 == 1
    c0 = jnp.where(upper, pltpu.roll(a[2], 64, 1), a[0])
    c2 = jnp.where(upper, a[2], pltpu.roll(a[0], 64, 1))
    c1 = jnp.where(upper, pltpu.roll(a[3], 64, 1), a[1])
    c3 = jnp.where(upper, a[3], pltpu.roll(a[1], 64, 1))
    return (
        jnp.where(odd, pltpu.roll(c1, 32, 1), c0),
        jnp.where(odd, c1, pltpu.roll(c0, 96, 1)),
        jnp.where(odd, pltpu.roll(c3, 32, 1), c2),
        jnp.where(odd, c3, pltpu.roll(c2, 96, 1)),
    )


def tile_of(tm, sp):
    cx, cz, cy, core = tm // 4, tm % 4, sp // 2, sp % 2
    zhi = cz // 2
    zlo = (cz + 1) // 2 % 2
    a = cx + zlo * (7 - 2 * cx)
    b = cy + zhi * (7 - 2 * cy)
    return 2 * a + core, b


def device_of(xi, yi):
    a, core = xi // 2, xi % 2
    zlo, zhi = a // 4, yi // 4
    cx = a + zlo * (7 - 2 * a)
    cy = yi + zhi * (7 - 2 * yi)
    cz = zlo + zhi * (3 - 2 * zlo)
    return cx * 4 + cz, cy * 2 + core


def two_terms(a):
    head = a.astype(jnp.bfloat16)
    return head, (a - head.astype(F32)).astype(jnp.bfloat16)


def dot(a, head, rest):
    a_head, a_rest = two_terms(a)
    small = jnp.dot(a_rest, head, preferred_element_type=F32) + jnp.dot(a_head, rest, preferred_element_type=F32)
    return jnp.dot(a_head, head, preferred_element_type=F32) + small


def kernel(
    anum, cond, source_in, start_in, guess_in, classes_in, dft_in, back_in, trig_in, out,
    source, start, guess, classes, dft, back, dft0, dft1, back0, back1, trig, insem, send1, recv1, send2, recv2, cls_send, cls_recv, kap, wxm, wxp, wym, wyp, wzi, wzm, wzp, wc,
    u0, u1, u2, u3, acc, beta, tsem, ksend, krecv, hsend, hrecv, outsem,
):
    tm = lax.axis_index("tm")
    sp = lax.axis_index("space")
    me = tm * NSP + sp
    xi, yi = tile_of(tm, sp)
    tile = xi * 8 + yi

    planes = [[(tm // 4 + dx) % 4 * 4 + (tm + dz) % 4 for dz in range(4)] for dx in range(4)]
    places = [[(sp // 2 + dy) % 4 * 2 + (sp + dc) % 2 for dc in range(2)] for dy in range(4)]

    barrier = pltpu.get_barrier_semaphore()
    for dx, dz, dy, dc in OFFSETS:
        pl.semaphore_signal(barrier, inc=1, device_id=(planes[dx][dz], places[dy][dc]), device_id_type=MESH)

    zhi = tm % 4 // 2
    half_lanes = pl.ds(pl.multiple_of(zhi * 128, 128), 128)
    pair_rows = pl.ds(pl.multiple_of(xi // 2 * 32, 32), 32)
    pairs = [
        (source_in, source),
        (classes_in.at[:, pair_rows, half_lanes], classes),
        (trig_in, trig),
        (dft_in, dft),
        (back_in, back),
    ]
    loads = [pltpu.make_async_copy(a, b, insem.at[i]) for i, (a, b) in enumerate(pairs)]
    firsts = [
        pltpu.make_async_copy(start_in, start, insem.at[5]),
        pltpu.make_async_copy(guess_in, guess, insem.at[6]),
    ]
    for copy in loads:
        copy.start()

    @pl.when(tm == 0)
    def _():
        for copy in firsts:
            copy.start()


    low_x, high_x, low_y, high_y = xi > 0, xi < 15, yi > 0, yi < 7
    beside = {-1: low_x, 1: high_x}, {-1: low_y, 1: high_y}

    def here(dx, dy):
        if dx and dy:
            return jnp.logical_and(beside[0][dx], beside[1][dy])
        return beside[0][dx] if dx else beside[1][dy]

    def span(d, low, middle, high):
        return {-1: low, 0: middle, 1: high}[d]

    def halo(dx, dy):
        return (
            span(dx, pl.ds(0, DEPTH), pl.ds(DEPTH, 16), pl.ds(DEPTH + 16, DEPTH)),
            span(dy, pl.ds(36, 4), pl.ds(0, 32), pl.ds(32, 4)),
        )

    for dx, dy in SIDES:

        @pl.when(jnp.logical_not(here(dx, dy)))
        def _(dx=dx, dy=dy):
            xs, ys = halo(dx, dy)
            for ref in (kap, u0.at[0], u0.at[1], u3.at[0], u3.at[1]):
                ref[xs, :, ys, :] = jnp.zeros((xs.size, 2, ys.size, 128), F32)

    log_alpha = jnp.log(jnp.full((8, 128), anum[0].astype(F32) / 32.0, F32))
    alpha = anum[0].astype(F32) / 32.0
    n0 = (2 * tm).astype(F32)
    scales = [jnp.exp(log_alpha * (n0 + t) / STEPS) for t in range(2)]
    unscales = [jnp.exp(-log_alpha * (n0 + t) / STEPS) for t in range(2)]

    loads[1].wait()
    for core in range(2):
        parts = [
            classes[z, core * 16 + xt * 8 : core * 16 + xt * 8 + 8, :]
            for xt in range(2)
            for z in range(2)
        ]
        for j, value in enumerate(swap_groups(parts)):
            cls_send[core, j] = value

    loads[0].wait()

    @pl.when(tm == 0)
    def _():
        for copy in firsts:
            copy.wait()

        def correct(x, carry):
            rows = pl.ds(pl.multiple_of(x * 16, 16), 16)
            for z in range(2):
                source[0, z, rows, :] = source[0, z, rows, :] + (start[z, rows, :] - alpha * guess[z, rows, :])
            return carry

        lax.fori_loop(0, 16, correct, 0)

    def pack(x, carry):
        for xt in range(2):
            rows = pl.ds(pl.multiple_of(x * 16 + xt * 8, 8), 8)
            for h in range(2):
                lanes = slice(h * 128, h * 128 + 128)
                parts = []
                for t in range(2):
                    for z in range(2):
                        value = source[t, z, rows, lanes]
                        parts.append(value * scales[t])
                for j, value in enumerate(swap_groups(parts)):
                    at = pl.multiple_of((x * 8 + h * 4 + j) * 16 + xt * 8, 8)
                    send1[pl.ds(at, 8), :] = value
        return carry

    lax.fori_loop(0, 16, pack, 0)

    for copy in loads[2:]:
        copy.wait()
    dft0[...], dft1[...] = two_terms(dft[...])
    back0[...], back1[...] = two_terms(back[...])
    for j, (re, im) in enumerate(chebyshev_table(log_alpha, trig[0:8, :], trig[8:16, :])):
        beta[j, 0:1, :] = re[0:1]
        beta[j, 1:2, :] = im[0:1]
        beta[j, 2:3, :] = -im[0:1]
        beta[j, 3:4, :] = re[4:5]

    pl.semaphore_wait(barrier, NDEV - 1)

    def cls_go(k, carry):
        other = (sp + k) % NSP
        ocy, ocore = other // 2, other % 2
        j = ocy + zhi * (3 - 2 * ocy)
        pltpu.make_async_remote_copy(
            src_ref=cls_send.at[ocore, j],
            dst_ref=cls_recv.at[pl.ds(pl.multiple_of(sp * 8, 8), 8)],
            send_sem=tsem.at[4],
            recv_sem=tsem.at[5],
            device_id=(tm, other),
            device_id_type=MESH,
        ).start()
        return carry

    lax.fori_loop(1, NSP, cls_go, 0)

    def rows16(index):
        return pl.ds(pl.multiple_of(index * 16, 16), 16)

    tiles_x = [[tile_of(planes[dx][dz], sp)[0] - sp % 2 for dz in range(4)] for dx in range(4)]
    tiles_y = [[tile_of(planes[0][dz], places[dy][0])[1] for dz in range(4)] for dy in range(4)]
    for dx, dz, dy, dc in OFFSETS:
        other = (tiles_x[dx][dz] + (sp + dc) % 2) * 8 + tiles_y[dy][dz]
        pltpu.make_async_remote_copy(
            src_ref=send1.at[rows16(other)],
            dst_ref=recv1.at[rows16(me)],
            send_sem=tsem.at[0],
            recv_sem=tsem.at[1],
            device_id=(planes[dx][dz], places[dy][dc]),
            device_id_type=MESH,
        ).start()
    recv1[rows16(me), :] = send1[rows16(tile), :]
    mycy, mycore = sp // 2, sp % 2
    cls_recv[pl.ds(pl.multiple_of(sp * 8, 8), 8), :] = cls_send[mycore, mycy + zhi * (3 - 2 * mycy)]

    some = cls_recv.at[pl.ds(0, 56)]
    pltpu.make_async_copy(some, some, tsem.at[5]).wait()

    def conductivities(xx, carry):
        codes = cls_recv[pl.ds(xx, 8, stride=8), :]
        value = jnp.zeros((8, 128), F32)
        for level in range(8):
            value = jnp.where(codes == level, cond[level], value)
        full = jnp.concatenate([value] * 16, axis=0).T
        for xt in range(2):
            kap[DEPTH + xt * 8 + xx, :, 0:32, :] = full[xt * 64 : xt * 64 + 64].reshape(2, 32, 128)
        return carry

    lax.fori_loop(0, 8, conductivities, 0)

    def edge(dx, dy):
        return (
            span(dx, pl.ds(DEPTH, DEPTH), pl.ds(DEPTH, 16), pl.ds(16, DEPTH)),
            span(dy, pl.ds(0, 4), pl.ds(0, 32), pl.ds(28, 4)),
        )

    def exchange(ref, send, recv, act):
        for i, (dx, dy) in enumerate(SIDES):

            @pl.when(here(dx, dy))
            def _(i=i, dx=dx, dy=dy):
                xs, ys = edge(dx, dy)
                xd, yd = halo(-dx, -dy)
                back_at = SIDES.index((-dx, -dy))
                copy = pltpu.make_async_remote_copy(
                    src_ref=ref.at[xs, :, ys, :],
                    dst_ref=ref.at[xd, :, yd, :],
                    send_sem=send.at[i],
                    recv_sem=recv.at[back_at],
                    device_id=device_of(
                        jnp.clip(xi + dx, 0, 15) if dx else xi, jnp.clip(yi + dy, 0, 7) if dy else yi
                    ),
                    device_id_type=MESH,
                )
                if act == "start":
                    copy.start()
                else:
                    copy.wait_send()
                    xh, yh = halo(dx, dy)
                    got = ref.at[xh, :, yh, :]
                    pltpu.make_async_copy(got, got, recv.at[i]).wait()

    exchange(kap, ksend, krecv, "start")
    most = recv1.at[pl.ds(0, (NDEV - 1) * 16)]
    pltpu.make_async_copy(most, most, tsem.at[1]).wait()

    def forward(quad, carry):
        rows = []
        for i in range(4):
            cells = recv1[pl.ds(quad * 4 + i, 128, stride=16), :].T
            rows.append(jnp.concatenate([cells[:64], cells[64:]], axis=1))
        spectrum = dot(jnp.concatenate(rows, axis=0), dft0[...], dft1[...])
        for i in range(4):
            x = quad * 4 + i
            for z in range(2):
                at = i * 64 + z * 32
                re = spectrum[at : at + 32, 0:128]
                im = spectrum[at : at + 32, 128:256]
                u0[0, DEPTH + x, z, 0:32] = re
                u0[1, DEPTH + x, z, 0:32] = im
                acc[0, x, z] = beta[0, 0:1, :] * re + beta[0, 2:3, :] * im
                acc[1, x, z] = beta[0, 1:2, :] * re + beta[0, 3:4, :] * im
        return carry

    lax.fori_loop(0, 4, forward, 0)

    def swap(block, p, act):
        exchange((u0, u3)[block].at[p], hsend.at[block, p], hrecv.at[block, p], act)

    def chebyshev(block, p):
        begin = (u0, u3)[block]
        for m in range(BLOCK):
            now = (begin, u1, begin, u2)[m]
            old = (None, begin, u1, begin)[m]
            new = (u1, begin, u2, u3)[m]
            last = m == BLOCK - 1
            spare = BLOCK - 1 - m
            h = slice(0, 32 if last else 40)

            def sweep(step, carry, now=now, old=old, new=new, last=last, spare=spare, h=h):
                first = DEPTH - spare + step * UNROLL
                field = [[now[p, first + i, z] for z in range(2)] for i in range(-1, UNROLL + 1)]
                values = []
                for i in range(UNROLL):
                    x = first + i
                    below, mid, above = field[i], field[i + 1], field[i + 2]
                    for z in range(2):
                        other = mid[1 - z][h]
                        outer = pltpu.roll(other, 1 if z == 0 else 127, 1)
                        before = pltpu.roll(mid[z], 1, 0)[h]
                        after = pltpu.roll(mid[z], 39, 0)[h]
                        value = wc[x, z, h] * mid[z][h] + wzi[x, h] * other
                        value = value + (wxm[x, z, h] * below[z][h] + wxp[x, z, h] * above[z][h])
                        if old is not None:
                            value = value - old[p, x, z, h]
                        rest = wym[x, z, h] * before + wyp[x, z, h] * after
                        value = value + (rest + (wzm if z == 0 else wzp)[x, h] * outer)
                        values.append((x, z, mid[z][h], value))
                if last:
                    totals = []
                    for x, z, own, value in values:
                        terms = [u1[p, x, z, h], old[p, x, z, h], own, value]
                        for to in range(2):
                            at = 2 * p + to
                            total = beta[BLOCK * block + 1, at : at + 1, :] * terms[0]
                            for i in range(1, 4):
                                total = total + beta[BLOCK * block + 1 + i, at : at + 1, :] * terms[i]
                            totals.append((to, x, z, acc[to, x - DEPTH, z] + total))
                    for to, x, z, total in totals:
                        acc[to, x - DEPTH, z] = total
                if not last or block == 0:
                    for x, z, own, value in values:
                        new[p, x, z, h] = value
                return carry

            lax.fori_loop(0, (16 + 2 * spare) // UNROLL, sweep, 0)

    swap(0, 0, "start")
    swap(0, 1, "start")
    exchange(kap, ksend, krecv, "wait")

    row_at = lax.broadcasted_iota(jnp.int32, (40, 128), 0)
    pair_at = lax.broadcasted_iota(jnp.int32, (40, 128), 1) % 8
    one = jnp.ones((40, 128), F32)
    inside_low = jnp.where(low_y, 1.0, 0.0).astype(F32)
    inside_high = jnp.where(high_y, 1.0, 0.0).astype(F32)
    columns = jnp.where(row_at < 32, one, jnp.where(row_at < 36, one * inside_high, one * inside_low)) * (1.0 / 12.0)

    def weights(x, carry):
        total = [None, None]
        inside_x = jnp.logical_and(jnp.logical_or(x >= DEPTH, low_x), jnp.logical_or(x < DEPTH + 16, high_x))
        part = columns * jnp.where(inside_x, 1.0, 0.0).astype(F32)
        k = [kap[x, z] for z in range(2)]
        for z in range(2):
            low = (k[z] + kap[x - 1, z]) * part
            high = (k[z] + kap[x + 1, z]) * part
            wxm[x, z] = low
            wxp[x, z] = high
            before = (k[z] + pltpu.roll(k[z], 1, 0)) * part
            after = (k[z] + pltpu.roll(k[z], 39, 0)) * part
            wym[x, z] = before
            wyp[x, z] = after
            total[z] = (low + high) + (before + after)
        inside = (k[0] + k[1]) * part
        below = (k[0] + jnp.where(pair_at == 0, 0.0, pltpu.roll(k[1], 1, 1))) * part
        above = (k[1] + jnp.where(pair_at == 7, 0.0, pltpu.roll(k[0], 127, 1))) * part
        wzi[x] = inside
        wzm[x] = jnp.where(pair_at == 0, 0.0, below)
        wzp[x] = jnp.where(pair_at == 7, 0.0, above)
        wc[x, 0] = part * 24.0 - (total[0] + (inside + below))
        wc[x, 1] = part * 24.0 - (total[1] + (inside + above))
        return carry

    lax.fori_loop(1, 23, weights, 0)

    for block in range(2):
        for p in range(2):
            swap(block, p, "wait")
            chebyshev(block, p)
            if block == 0:
                swap(1, p, "start")

    def inverse(quad, carry):
        rows = []
        for i in range(4):
            x = quad * 4 + i
            rows.append(
                jnp.concatenate([acc[0, x].reshape(64, 128), acc[1, x].reshape(64, 128)], axis=1)
            )
        times = dot(jnp.concatenate(rows, axis=0), back0[...], back1[...])
        for i in range(4):
            own = times[i * 64 : i * 64 + 64]
            cells = jnp.concatenate([own[:, :128], own[:, 128:]], axis=0)
            send2[pl.ds(quad * 4 + i, 128, stride=16), :] = cells.T
        return carry

    lax.fori_loop(0, 4, inverse, 0)

    for dx, dz, dy, dc in OFFSETS:
        pltpu.make_async_remote_copy(
            src_ref=send2.at[rows16(planes[dx][dz] * NSP + places[dy][dc])],
            dst_ref=recv2.at[rows16(tile)],
            send_sem=tsem.at[2],
            recv_sem=tsem.at[3],
            device_id=(planes[dx][dz], places[dy][dc]),
            device_id_type=MESH,
        ).start()
    recv2[rows16(tile), :] = send2[rows16(me), :]
    most2 = recv2.at[pl.ds(0, (NDEV - 1) * 16)]
    pltpu.make_async_copy(most2, most2, tsem.at[3]).wait()

    def unpack(x, carry):
        for xt in range(2):
            rows = pl.ds(pl.multiple_of(x * 16 + xt * 8, 8), 8)
            for h in range(2):
                parts = [
                    recv2[pl.ds(pl.multiple_of((x * 8 + h * 4 + j) * 16 + xt * 8, 8), 8), :]
                    for j in range(4)
                ]
                for i, value in enumerate(swap_groups(parts)):
                    source[i // 2, i % 2, rows, h * 128 : h * 128 + 128] = value * unscales[i // 2]
        rows = pl.ds(pl.multiple_of(x * 16, 16), 16)
        pltpu.make_async_copy(source.at[:, :, rows, :], out.at[:, :, rows, :], outsem).start()
        return carry

    lax.fori_loop(0, 16, unpack, 0)

    pltpu.make_async_copy(most, most, tsem.at[0]).wait()
    pltpu.make_async_copy(most2, most2, tsem.at[2]).wait()
    pltpu.make_async_copy(some, some, tsem.at[4]).wait()
    pltpu.make_async_copy(source, out, outsem).wait()


def body(source, start_field, last_guess, classes, conductivity, alpha_num):
    consts = [jnp.asarray(t) for t in tables()]
    smem = pl.BlockSpec(memory_space=pltpu.SMEM)
    hbm = pl.BlockSpec(memory_space=pltpu.HBM)
    BF16 = jnp.bfloat16
    V = pltpu.VMEM
    return pl.pallas_call(
        kernel,
        out_shape=jax.ShapeDtypeStruct((2, 2, 256, 256), F32),
        in_specs=[smem, smem] + [hbm] * 7,
        out_specs=hbm,
        scratch_shapes=[
            V((2, 2, 256, 256), F32), V((2, 256, 256), F32), V((2, 256, 256), F32), V((2, 32, 128), jnp.int32),
            V((256, 256), F32), V((256, 256), F32), V((256, 256), BF16), V((256, 256), BF16), V((256, 256), BF16), V((256, 256), BF16), V((16, 128), F32),
            pltpu.SemaphoreType.DMA((7,)),
            V((2048, 128), F32), V((2048, 128), F32), V((2048, 128), F32), V((2048, 128), F32),
            V((2, 4, 8, 128), jnp.int32), V((64, 128), jnp.int32),
            V((24, 2, 40, 128), F32), V((24, 2, 40, 128), F32), V((24, 2, 40, 128), F32), V((24, 2, 40, 128), F32),
            V((24, 2, 40, 128), F32),
            V((24, 40, 128), F32), V((24, 40, 128), F32), V((24, 40, 128), F32), V((24, 2, 40, 128), F32),
            V((2, 24, 2, 40, 128), F32), V((2, 24, 2, 40, 128), F32), V((2, 24, 2, 40, 128), F32), V((2, 24, 2, 40, 128), F32), V((2, 16, 2, 32, 128), F32), V((CHEB + 1, 8, 128), F32),
            pltpu.SemaphoreType.DMA((6,)),
            pltpu.SemaphoreType.DMA((8,)), pltpu.SemaphoreType.DMA((8,)),
            pltpu.SemaphoreType.DMA((2, 2, 8)), pltpu.SemaphoreType.DMA((2, 2, 8)), pltpu.SemaphoreType.DMA,
        ],
        compiler_params=pltpu.CompilerParams(
            collective_id=1, has_side_effects=True, vmem_limit_bytes=62 * 2**20
        ),
    )(alpha_num, conductivity, source, start_field, last_guess, classes, *consts)


def solution(mesh):
    placed = (
        P("tm", "space", None, None),
        P("space", None, None),
        P("space", None, None),
        P("space", None, None),
        P(),
        P(),
    )
    return jax.shard_map(
        body, mesh=mesh, in_specs=placed, out_specs=P("tm", "space", None, None), check_vma=False
    )
```

```python
import functools

import jax
import jax.numpy as jnp
import numpy as np
from jax import lax
from jax.experimental import pallas as pl
from jax.experimental.pallas import tpu as pltpu
from jax.sharding import PartitionSpec as P

MESH = pl.DeviceIdType.MESH
F32 = jnp.float32
CHEB = 8
STEPS = 32
HALF_SPAN = 12.0
NTM, NSP = 16, 8
NDEV = NTM * NSP
OFFSETS = sorted(
    [(dx, dz, dy, dc) for dx in range(4) for dz in range(4) for dy in range(4) for dc in range(2)][1:],
    key=lambda o: -sum(min(d, 4 - d) for d in o[:3]),
)
DEPTH = 4
BLOCK = 4
UNROLL = 8
SIDES = [(dx, dy) for dx in (-1, 0, 1) for dy in (-1, 0, 1) if (dx, dy) != (0, 0)]


def tables():
    lane = np.arange(128)
    slot, pair = lane // 8, lane % 8
    dft = np.zeros((2, 128, 2, 128))
    back = np.zeros((2, 128, 2, 128))
    same = (pair[:, None] == pair[None, :]).astype(np.float64)
    for half in range(2):
        n = 2 * slot + half
        angle = 2 * np.pi * ((n[:, None] * slot[None, :]) % STEPS) / STEPS
        sign = np.where(n % 2 == 0, 1.0, -1.0)[:, None]
        first = (slot == 0)[None, :]
        real = np.cos(angle)
        imag = np.where(first, sign, -np.sin(angle))
        weight = np.where(first, 1.0, 2.0) / STEPS
        dft[half, :, 0, :] = same * real
        dft[half, :, 1, :] = same * imag
        back[0, :, half, :] = (same * real * weight).T
        back[1, :, half, :] = (same * imag * weight).T
    trig = np.zeros((16, 128))
    for row in range(8):
        freq = np.where((slot == 0) & (row >= 4), 16, slot)
        angle = 2 * np.pi * freq / STEPS
        trig[row] = np.cos(angle)
        trig[8 + row] = np.where(slot == 0, 0.0, np.sin(angle))
    return (
        dft.reshape(256, 256).astype(np.float32),
        back.reshape(256, 256).astype(np.float32),
        trig.astype(np.float32),
    )


def cmul(a, b):
    return (a[0] * b[0] - a[1] * b[1], a[0] * b[1] + a[1] * b[0])


def cinv(a):
    denom = a[0] * a[0] + a[1] * a[1]
    return (a[0] / denom, -a[1] / denom)


def chebyshev_table(log_alpha, cos_f, sin_f):
    ratio = jnp.exp(log_alpha / STEPS)
    center = (1.0 - ratio * cos_f + HALF_SPAN, ratio * sin_f)
    sigma = (center[0] / HALF_SPAN, center[1] / HALF_SPAN)
    rho = [cinv(sigma)]
    for _ in range(CHEB):
        rho.append(cinv((2.0 * sigma[0] - rho[-1][0], 2.0 * sigma[1] - rho[-1][1])))
    inner = (jnp.ones_like(cos_f), jnp.zeros_like(cos_f))
    gains = [None] * (CHEB + 1)
    for j in range(CHEB, -1, -1):
        if j < CHEB:
            step = cmul(cmul(rho[j + 1], rho[j]), inner)
            inner = (1.0 + step[0], step[1])
        scale = cinv(center) if j == 0 else (rho[j][0] / 6.0, rho[j][1] / 6.0)
        gains[j] = cmul(scale, inner)
    level = (jnp.ones_like(cos_f), jnp.zeros_like(cos_f))
    terms = []
    for j in range(CHEB + 1):
        terms.append(cmul(gains[j], level))
        level = cmul(level, rho[j])
    zero = (jnp.zeros_like(cos_f), jnp.zeros_like(cos_f))
    terms += [zero, zero]
    out = []
    for j in range(CHEB + 1):
        own = terms[j] if j == 0 else (0.5 * terms[j][0], 0.5 * terms[j][1])
        out.append((own[0] - 0.5 * terms[j + 2][0], own[1] - 0.5 * terms[j + 2][1]))
    for m in range(BLOCK, 0, -1):
        for j in range(BLOCK + m - 2, BLOCK - m - 1, -2):
            out[j] = (out[j][0] - out[BLOCK + m][0], out[j][1] - out[BLOCK + m][1])
    return out


def swap_groups(a):
    group = lax.broadcasted_iota(jnp.int32, a[0].shape, 1) // 32
    upper = group >= 2
    odd = group % 2 == 1
    c0 = jnp.where(upper, pltpu.roll(a[2], 64, 1), a[0])
    c2 = jnp.where(upper, a[2], pltpu.roll(a[0], 64, 1))
    c1 = jnp.where(upper, pltpu.roll(a[3], 64, 1), a[1])
    c3 = jnp.where(upper, a[3], pltpu.roll(a[1], 64, 1))
    return (
        jnp.where(odd, pltpu.roll(c1, 32, 1), c0),
        jnp.where(odd, c1, pltpu.roll(c0, 96, 1)),
        jnp.where(odd, pltpu.roll(c3, 32, 1), c2),
        jnp.where(odd, c3, pltpu.roll(c2, 96, 1)),
    )


def tile_of(tm, sp):
    cx, cz, cy, core = tm // 4, tm % 4, sp // 2, sp % 2
    zhi = cz // 2
    zlo = (cz + 1) // 2 % 2
    a = cx + zlo * (7 - 2 * cx)
    b = cy + zhi * (7 - 2 * cy)
    return 2 * a + core, b


def device_of(xi, yi):
    a, core = xi // 2, xi % 2
    zlo, zhi = a // 4, yi // 4
    cx = a + zlo * (7 - 2 * a)
    cy = yi + zhi * (7 - 2 * yi)
    cz = zlo + zhi * (3 - 2 * zlo)
    return cx * 4 + cz, cy * 2 + core


def two_terms(a):
    head = a.astype(jnp.bfloat16)
    return head, (a - head.astype(F32)).astype(jnp.bfloat16)


def dot(a, head, rest):
    a_head, a_rest = two_terms(a)
    small = jnp.dot(a_rest, head, preferred_element_type=F32) + jnp.dot(a_head, rest, preferred_element_type=F32)
    return jnp.dot(a_head, head, preferred_element_type=F32) + small


def kernel(
    anum, cond, source_in, start_in, guess_in, classes_in, dft_in, back_in, trig_in, recv2,
    source, start, guess, classes, dft, back, dft0, dft1, back0, back1, trig, insem, send1, recv1, send2, cls_send, cls_recv, kap, wxm, wxp, wym, wyp, wzi, wzm, wzp, wc,
    u0, u1, u2, u3, acc, beta, tsem, ksend, krecv, hsend, hrecv, selfsem,
):
    tm = lax.axis_index("tm")
    sp = lax.axis_index("space")
    me = tm * NSP + sp
    xi, yi = tile_of(tm, sp)
    tile = xi * 8 + yi

    planes = [[(tm // 4 + dx) % 4 * 4 + (tm + dz) % 4 for dz in range(4)] for dx in range(4)]
    places = [[(sp // 2 + dy) % 4 * 2 + (sp + dc) % 2 for dc in range(2)] for dy in range(4)]

    zhi = tm % 4 // 2
    half_lanes = pl.ds(pl.multiple_of(zhi * 128, 128), 128)
    pair_rows = pl.ds(pl.multiple_of(xi // 2 * 32, 32), 32)
    pairs = [
        (source_in, source),
        (classes_in.at[:, pair_rows, half_lanes], classes),
        (trig_in, trig),
        (dft_in, dft),
        (back_in, back),
    ]
    loads = [pltpu.make_async_copy(a, b, insem.at[i]) for i, (a, b) in enumerate(pairs)]
    firsts = [
        pltpu.make_async_copy(start_in, start, insem.at[5]),
        pltpu.make_async_copy(guess_in, guess, insem.at[6]),
    ]
    for copy in loads:
        copy.start()

    @pl.when(tm == 0)
    def _():
        for copy in firsts:
            copy.start()


    barrier = pltpu.get_barrier_semaphore()
    for dx, dz, dy, dc in OFFSETS:
        pl.semaphore_signal(barrier, inc=1, device_id=(planes[dx][dz], places[dy][dc]), device_id_type=MESH)

    low_x, high_x, low_y, high_y = xi > 0, xi < 15, yi > 0, yi < 7
    beside = {-1: low_x, 1: high_x}, {-1: low_y, 1: high_y}

    def here(dx, dy):
        if dx and dy:
            return jnp.logical_and(beside[0][dx], beside[1][dy])
        return beside[0][dx] if dx else beside[1][dy]

    def span(d, low, middle, high):
        return {-1: low, 0: middle, 1: high}[d]

    def halo(dx, dy):
        return (
            span(dx, pl.ds(0, DEPTH), pl.ds(DEPTH, 16), pl.ds(DEPTH + 16, DEPTH)),
            span(dy, pl.ds(36, 4), pl.ds(0, 32), pl.ds(32, 4)),
        )

    log_alpha = jnp.log(jnp.full((8, 128), anum[0].astype(F32) / 32.0, F32))
    alpha = anum[0].astype(F32) / 32.0
    n0 = (2 * tm).astype(F32)
    scales = [jnp.exp(log_alpha * (n0 + t) / STEPS) for t in range(2)]

    loads[0].wait()

    @pl.when(tm == 0)
    def _():
        for copy in firsts:
            copy.wait()

        def correct(x, carry):
            rows = pl.ds(pl.multiple_of(x * 16, 16), 16)
            for z in range(2):
                source[0, z, rows, :] = source[0, z, rows, :] + (start[z, rows, :] - alpha * guess[z, rows, :])
            return carry

        lax.fori_loop(0, 16, correct, 0)

    def pack(step, carry):
        todo = []
        for x, xt in [(2 * step + i, xt) for i in range(2) for xt in range(2)]:
            rows = pl.ds(pl.multiple_of(x * 16 + xt * 8, 8), 8)
            for h in range(2):
                lanes = slice(h * 128, h * 128 + 128)
                parts = []
                for t in range(2):
                    for z in range(2):
                        value = source[t, z, rows, lanes]
                        parts.append(value * scales[t])
                for j, value in enumerate(swap_groups(parts)):
                    at = pl.multiple_of((x * 8 + h * 4 + j) * 16 + xt * 8, 8)
                    todo.append((at, value))
        for at, value in todo:
            send1[pl.ds(at, 8), :] = value
        return carry

    lax.fori_loop(0, 8, pack, 0)

    loads[1].wait()
    for core in range(2):
        parts = [
            classes[z, core * 16 + xt * 8 : core * 16 + xt * 8 + 8, :]
            for xt in range(2)
            for z in range(2)
        ]
        for j, value in enumerate(swap_groups(parts)):
            cls_send[core, j] = value

    pl.semaphore_wait(barrier, NDEV - 1)

    def cls_go(k, carry):
        other = (sp + k) % NSP
        ocy, ocore = other // 2, other % 2
        j = ocy + zhi * (3 - 2 * ocy)
        pltpu.make_async_remote_copy(
            src_ref=cls_send.at[ocore, j],
            dst_ref=cls_recv.at[pl.ds(pl.multiple_of(sp * 8, 8), 8)],
            send_sem=tsem.at[4],
            recv_sem=tsem.at[5],
            device_id=(tm, other),
            device_id_type=MESH,
        ).start()
        return carry

    lax.fori_loop(1, NSP, cls_go, 0)

    def rows16(index):
        return pl.ds(pl.multiple_of(index * 16, 16), 16)

    tiles_x = [[tile_of(planes[dx][dz], sp)[0] - sp % 2 for dz in range(4)] for dx in range(4)]
    tiles_y = [[tile_of(planes[0][dz], places[dy][0])[1] for dz in range(4)] for dy in range(4)]
    for dx, dz, dy, dc in OFFSETS:
        other = (tiles_x[dx][dz] + (sp + dc) % 2) * 8 + tiles_y[dy][dz]
        pltpu.make_async_remote_copy(
            src_ref=send1.at[rows16(other)],
            dst_ref=recv1.at[rows16(me)],
            send_sem=tsem.at[0],
            recv_sem=tsem.at[1],
            device_id=(planes[dx][dz], places[dy][dc]),
            device_id_type=MESH,
        ).start()
    recv1[rows16(me), :] = send1[rows16(tile), :]
    mycy, mycore = sp // 2, sp % 2
    cls_recv[pl.ds(pl.multiple_of(sp * 8, 8), 8), :] = cls_send[mycore, mycy + zhi * (3 - 2 * mycy)]

    for copy in loads[2:]:
        copy.wait()
    dft0[...], dft1[...] = two_terms(dft[...])
    back0[...], back1[...] = two_terms(back[...])
    for j, (re, im) in enumerate(chebyshev_table(log_alpha, trig[0:8, :], trig[8:16, :])):
        beta[j, 0:1, :] = re[0:1]
        beta[j, 1:2, :] = im[0:1]
        beta[j, 2:3, :] = -im[0:1]
        beta[j, 3:4, :] = re[4:5]

    for dx, dy in SIDES:

        @pl.when(jnp.logical_not(here(dx, dy)))
        def _(dx=dx, dy=dy):
            xs, ys = halo(dx, dy)
            for ref in (kap, u0.at[0], u0.at[1], u3.at[0], u3.at[1]):
                ref[xs, :, ys, :] = jnp.zeros((xs.size, 2, ys.size, 128), F32)

    some = cls_recv.at[pl.ds(0, 56)]
    pltpu.make_async_copy(some, some, tsem.at[5]).wait()

    def conductivities(xx, carry):
        codes = cls_recv[pl.ds(xx, 8, stride=8), :]
        value = jnp.zeros((8, 128), F32)
        for level in range(8):
            value = jnp.where(codes == level, cond[level], value)
        full = jnp.concatenate([value] * 16, axis=0).T
        for xt in range(2):
            kap[DEPTH + xt * 8 + xx, :, 0:32, :] = full[xt * 64 : xt * 64 + 64].reshape(2, 32, 128)
        return carry

    lax.fori_loop(0, 8, conductivities, 0)

    def edge(dx, dy):
        return (
            span(dx, pl.ds(DEPTH, DEPTH), pl.ds(DEPTH, 16), pl.ds(16, DEPTH)),
            span(dy, pl.ds(0, 4), pl.ds(0, 32), pl.ds(28, 4)),
        )

    def exchange(ref, send, recv, act):
        for i, (dx, dy) in enumerate(SIDES):

            @pl.when(here(dx, dy))
            def _(i=i, dx=dx, dy=dy):
                xs, ys = edge(dx, dy)
                xd, yd = halo(-dx, -dy)
                back_at = SIDES.index((-dx, -dy))
                copy = pltpu.make_async_remote_copy(
                    src_ref=ref.at[xs, :, ys, :],
                    dst_ref=ref.at[xd, :, yd, :],
                    send_sem=send.at[i],
                    recv_sem=recv.at[back_at],
                    device_id=device_of(
                        jnp.clip(xi + dx, 0, 15) if dx else xi, jnp.clip(yi + dy, 0, 7) if dy else yi
                    ),
                    device_id_type=MESH,
                )
                if act == "start":
                    copy.start()
                else:
                    copy.wait_send()
                    xh, yh = halo(dx, dy)
                    got = ref.at[xh, :, yh, :]
                    pltpu.make_async_copy(got, got, recv.at[i]).wait()

    exchange(kap, ksend, krecv, "start")
    most = recv1.at[pl.ds(0, (NDEV - 1) * 16)]
    pltpu.make_async_copy(most, most, tsem.at[1]).wait()

    def forward(quad, carry):
        rows = []
        for i in range(4):
            cells = recv1[pl.ds(quad * 4 + i, 128, stride=16), :].T
            rows.append(jnp.concatenate([cells[:64], cells[64:]], axis=1))
        spectrum = dot(jnp.concatenate(rows, axis=0), dft0[...], dft1[...])
        for i in range(4):
            x = quad * 4 + i
            for z in range(2):
                at = i * 64 + z * 32
                re = spectrum[at : at + 32, 0:128]
                im = spectrum[at : at + 32, 128:256]
                u0[0, DEPTH + x, z, 0:32] = re
                u0[1, DEPTH + x, z, 0:32] = im
                acc[0, x, z] = beta[0, 0:1, :] * re + beta[0, 2:3, :] * im
                acc[1, x, z] = beta[0, 1:2, :] * re + beta[0, 3:4, :] * im
        return carry

    lax.fori_loop(0, 4, forward, 0)

    def swap(block, p, act):
        exchange((u0, u3)[block].at[p], hsend.at[block, p], hrecv.at[block, p], act)

    def chebyshev(block, p):
        begin = (u0, u3)[block]
        for m in range(BLOCK):
            now = (begin, u1, begin, u2)[m]
            old = (None, begin, u1, begin)[m]
            new = (u1, begin, u2, u3)[m]
            last = m == BLOCK - 1
            spare = BLOCK - 1 - m
            h = slice(0, 32 if last else 40)

            def sweep(first, count, now=now, old=old, new=new, last=last, h=h):
                field = [[now[p, first + i, z] for z in range(2)] for i in range(-1, count + 1)]
                values = []
                for i in range(count):
                    x = first + i
                    below, mid, above = field[i], field[i + 1], field[i + 2]
                    for z in range(2):
                        other = mid[1 - z][h]
                        outer = pltpu.roll(other, 1 if z == 0 else 127, 1)
                        before = pltpu.roll(mid[z], 1, 0)[h]
                        after = pltpu.roll(mid[z], 39, 0)[h]
                        value = wc[x, z, h] * mid[z][h] + wzi[x, h] * other
                        value = value + (wxm[x, z, h] * below[z][h] + wxp[x, z, h] * above[z][h])
                        if old is not None:
                            value = value - old[p, x, z, h]
                        rest = wym[x, z, h] * before + wyp[x, z, h] * after
                        value = value + (rest + (wzm if z == 0 else wzp)[x, h] * outer)
                        values.append((x, z, mid[z][h], value))
                if last:
                    totals = []
                    for x, z, own, value in values:
                        terms = [u1[p, x, z, h], old[p, x, z, h], own, value]
                        for to in range(2):
                            at = 2 * p + to
                            total = beta[BLOCK * block + 1, at : at + 1, :] * terms[0]
                            for i in range(1, 4):
                                total = total + beta[BLOCK * block + 1 + i, at : at + 1, :] * terms[i]
                            totals.append((to, x, z, acc[to, x - DEPTH, z] + total))
                    for to, x, z, total in totals:
                        acc[to, x - DEPTH, z] = total
                if not last or block == 0:
                    for x, z, own, value in values:
                        new[p, x, z, h] = value

            steps, rest = divmod(16 + 2 * spare, UNROLL)

            def several(step, carry, sweep=sweep, spare=spare):
                sweep(DEPTH - spare + step * UNROLL, UNROLL)
                return carry

            lax.fori_loop(0, steps, several, 0)
            if rest:
                sweep(DEPTH - spare + steps * UNROLL, rest)

    swap(0, 0, "start")
    swap(0, 1, "start")
    exchange(kap, ksend, krecv, "wait")

    row_at = lax.broadcasted_iota(jnp.int32, (40, 128), 0)
    pair_at = lax.broadcasted_iota(jnp.int32, (40, 128), 1) % 8
    one = jnp.ones((40, 128), F32)
    inside_low = jnp.where(low_y, 1.0, 0.0).astype(F32)
    inside_high = jnp.where(high_y, 1.0, 0.0).astype(F32)
    columns = jnp.where(row_at < 32, one, jnp.where(row_at < 36, one * inside_high, one * inside_low)) * (1.0 / 12.0)

    def weights(x, carry):
        total = [None, None]
        inside_x = jnp.logical_and(jnp.logical_or(x >= DEPTH, low_x), jnp.logical_or(x < DEPTH + 16, high_x))
        part = columns * jnp.where(inside_x, 1.0, 0.0).astype(F32)
        k = [kap[x, z] for z in range(2)]
        for z in range(2):
            low = (k[z] + kap[x - 1, z]) * part
            high = (k[z] + kap[x + 1, z]) * part
            wxm[x, z] = low
            wxp[x, z] = high
            before = (k[z] + pltpu.roll(k[z], 1, 0)) * part
            after = (k[z] + pltpu.roll(k[z], 39, 0)) * part
            wym[x, z] = before
            wyp[x, z] = after
            total[z] = (low + high) + (before + after)
        inside = (k[0] + k[1]) * part
        below = (k[0] + jnp.where(pair_at == 0, 0.0, pltpu.roll(k[1], 1, 1))) * part
        above = (k[1] + jnp.where(pair_at == 7, 0.0, pltpu.roll(k[0], 127, 1))) * part
        wzi[x] = inside
        wzm[x] = jnp.where(pair_at == 0, 0.0, below)
        wzp[x] = jnp.where(pair_at == 7, 0.0, above)
        wc[x, 0] = part * 24.0 - (total[0] + (inside + below))
        wc[x, 1] = part * 24.0 - (total[1] + (inside + above))
        return carry

    lax.fori_loop(1, 23, weights, 0)

    for block in range(2):
        for p in range(2):
            swap(block, p, "wait")
            chebyshev(block, p)
            if block == 0:
                swap(1, p, "start")

    def inverse(quad, carry):
        rows = []
        for i in range(4):
            x = quad * 4 + i
            rows.append(
                jnp.concatenate([acc[0, x].reshape(64, 128), acc[1, x].reshape(64, 128)], axis=1)
            )
        times = dot(jnp.concatenate(rows, axis=0), back0[...], back1[...])
        for i in range(4):
            own = times[i * 64 : i * 64 + 64]
            cells = jnp.concatenate([own[:, :128], own[:, 128:]], axis=0)
            send2[pl.ds(quad * 4 + i, 128, stride=16), :] = cells.T
        return carry

    lax.fori_loop(0, 4, inverse, 0)

    for dx, dz, dy, dc in OFFSETS:
        pltpu.make_async_remote_copy(
            src_ref=send2.at[rows16(planes[dx][dz] * NSP + places[dy][dc])],
            dst_ref=recv2.at[rows16(tile)],
            send_sem=tsem.at[2],
            recv_sem=tsem.at[3],
            device_id=(planes[dx][dz], places[dy][dc]),
            device_id_type=MESH,
        ).start()
    own = pltpu.make_async_copy(send2.at[rows16(me)], recv2.at[rows16(tile)], selfsem)
    own.start()
    own.wait()
    most2 = recv2.at[pl.ds(0, (NDEV - 1) * 16)]
    pltpu.make_async_copy(most2, most2, tsem.at[3]).wait()

    pltpu.make_async_copy(most, most, tsem.at[0]).wait()
    pltpu.make_async_copy(most2, most2, tsem.at[2]).wait()
    pltpu.make_async_copy(some, some, tsem.at[4]).wait()


def unpack_kernel(anum, tiles, out):
    log_alpha = jnp.log(jnp.full((8, 128), anum[0].astype(F32) / 32.0, F32))
    n0 = (2 * lax.axis_index("tm")).astype(F32)
    unscales = [jnp.exp(-log_alpha * (n0 + t) / STEPS) for t in range(2)]
    for x in range(out.shape[2] // 16):
        todo = []
        for xt in range(2):
            row = x * 16 + xt * 8
            for h in range(2):
                parts = [tiles[(x * 8 + h * 4 + j) * 16 + xt * 8 : (x * 8 + h * 4 + j) * 16 + xt * 8 + 8, :] for j in range(4)]
                for i, value in enumerate(swap_groups(parts)):
                    todo.append((i // 2, i % 2, row, h * 128, value * unscales[i // 2]))
        for t, z, row, lane, value in todo:
            out[t, z, row : row + 8, lane : lane + 128] = value


def body(source, start_field, last_guess, classes, conductivity, alpha_num):
    consts = [jnp.asarray(t) for t in tables()]
    smem = pl.BlockSpec(memory_space=pltpu.SMEM)
    hbm = pl.BlockSpec(memory_space=pltpu.HBM)
    BF16 = jnp.bfloat16
    V = pltpu.VMEM
    tiles = pl.pallas_call(
        kernel,
        out_shape=jax.ShapeDtypeStruct((2048, 128), F32),
        in_specs=[smem, smem] + [hbm] * 7,
        out_specs=hbm,
        scratch_shapes=[
            V((2, 2, 256, 256), F32), V((2, 256, 256), F32), V((2, 256, 256), F32), V((2, 32, 128), jnp.int32),
            V((256, 256), F32), V((256, 256), F32), V((256, 256), BF16), V((256, 256), BF16), V((256, 256), BF16), V((256, 256), BF16), V((16, 128), F32),
            pltpu.SemaphoreType.DMA((7,)),
            V((2048, 128), F32), V((2048, 128), F32), V((2048, 128), F32),
            V((2, 4, 8, 128), jnp.int32), V((64, 128), jnp.int32),
            V((24, 2, 40, 128), F32), V((24, 2, 40, 128), F32), V((24, 2, 40, 128), F32), V((24, 2, 40, 128), F32),
            V((24, 2, 40, 128), F32),
            V((24, 40, 128), F32), V((24, 40, 128), F32), V((24, 40, 128), F32), V((24, 2, 40, 128), F32),
            V((2, 24, 2, 40, 128), F32), V((2, 24, 2, 40, 128), F32), V((2, 24, 2, 40, 128), F32), V((2, 24, 2, 40, 128), F32), V((2, 16, 2, 32, 128), F32), V((CHEB + 1, 8, 128), F32),
            pltpu.SemaphoreType.DMA((6,)),
            pltpu.SemaphoreType.DMA((8,)), pltpu.SemaphoreType.DMA((8,)),
            pltpu.SemaphoreType.DMA((2, 2, 8)), pltpu.SemaphoreType.DMA((2, 2, 8)), pltpu.SemaphoreType.DMA,
        ],
        compiler_params=pltpu.CompilerParams(
            collective_id=1, has_side_effects=True, vmem_limit_bytes=62 * 2**20
        ),
    )(alpha_num, conductivity, source, start_field, last_guess, classes, *consts)
    steps = 4
    return pl.pallas_call(
        unpack_kernel,
        grid=(steps,),
        out_shape=jax.ShapeDtypeStruct((2, 2, 256, 256), F32),
        in_specs=[smem, pl.BlockSpec((2048 // steps, 128), lambda i: (i, 0))],
        out_specs=pl.BlockSpec((2, 2, 256 // steps, 256), lambda i: (0, 0, i, 0)),
    )(alpha_num, tiles)


def solution(mesh):
    placed = (
        P("tm", "space", None, None),
        P("space", None, None),
        P("space", None, None),
        P("space", None, None),
        P(),
        P(),
    )
    return jax.shard_map(
        body, mesh=mesh, in_specs=placed, out_specs=P("tm", "space", None, None), check_vma=False
    )
```

```python
import functools

import jax
import jax.numpy as jnp
import numpy as np
from jax import lax
from jax.experimental import pallas as pl
from jax.experimental.pallas import tpu as pltpu
from jax.sharding import PartitionSpec as P

MESH = pl.DeviceIdType.MESH
F32 = jnp.float32
CHEB = 8
STEPS = 32
HALF_SPAN = 12.0
NTM, NSP = 16, 8
NDEV = NTM * NSP
OFFSETS = sorted(
    [(dx, dz, dy, dc) for dx in range(4) for dz in range(4) for dy in range(4) for dc in range(2)][1:],
    key=lambda o: -sum(min(d, 4 - d) for d in o[:3]),
)
DEPTH = 4
BLOCK = 4
UNROLL = 8
SIDES = [(dx, dy) for dx in (-1, 0, 1) for dy in (-1, 0, 1) if (dx, dy) != (0, 0)]


def tables():
    lane = np.arange(128)
    slot, pair = lane // 8, lane % 8
    dft = np.zeros((2, 128, 2, 128))
    back = np.zeros((2, 128, 2, 128))
    same = (pair[:, None] == pair[None, :]).astype(np.float64)
    for half in range(2):
        n = 2 * slot + half
        angle = 2 * np.pi * ((n[:, None] * slot[None, :]) % STEPS) / STEPS
        sign = np.where(n % 2 == 0, 1.0, -1.0)[:, None]
        first = (slot == 0)[None, :]
        real = np.cos(angle)
        imag = np.where(first, sign, -np.sin(angle))
        weight = np.where(first, 1.0, 2.0) / STEPS
        dft[half, :, 0, :] = same * real
        dft[half, :, 1, :] = same * imag
        back[0, :, half, :] = (same * real * weight).T
        back[1, :, half, :] = (same * imag * weight).T
    trig = np.zeros((16, 128))
    for row in range(8):
        freq = np.where((slot == 0) & (row >= 4), 16, slot)
        angle = 2 * np.pi * freq / STEPS
        trig[row] = np.cos(angle)
        trig[8 + row] = np.where(slot == 0, 0.0, np.sin(angle))
    return (
        dft.reshape(256, 256).astype(np.float32),
        back.reshape(256, 256).astype(np.float32),
        trig.astype(np.float32),
    )


def cmul(a, b):
    return (a[0] * b[0] - a[1] * b[1], a[0] * b[1] + a[1] * b[0])


def cinv(a):
    denom = a[0] * a[0] + a[1] * a[1]
    return (a[0] / denom, -a[1] / denom)


def chebyshev_table(log_alpha, cos_f, sin_f):
    ratio = jnp.exp(log_alpha / STEPS)
    center = (1.0 - ratio * cos_f + HALF_SPAN, ratio * sin_f)
    sigma = (center[0] / HALF_SPAN, center[1] / HALF_SPAN)
    rho = [cinv(sigma)]
    for _ in range(CHEB):
        rho.append(cinv((2.0 * sigma[0] - rho[-1][0], 2.0 * sigma[1] - rho[-1][1])))
    inner = (jnp.ones_like(cos_f), jnp.zeros_like(cos_f))
    gains = [None] * (CHEB + 1)
    for j in range(CHEB, -1, -1):
        if j < CHEB:
            step = cmul(cmul(rho[j + 1], rho[j]), inner)
            inner = (1.0 + step[0], step[1])
        scale = cinv(center) if j == 0 else (rho[j][0] / 6.0, rho[j][1] / 6.0)
        gains[j] = cmul(scale, inner)
    level = (jnp.ones_like(cos_f), jnp.zeros_like(cos_f))
    terms = []
    for j in range(CHEB + 1):
        terms.append(cmul(gains[j], level))
        level = cmul(level, rho[j])
    zero = (jnp.zeros_like(cos_f), jnp.zeros_like(cos_f))
    terms += [zero, zero]
    out = []
    for j in range(CHEB + 1):
        own = terms[j] if j == 0 else (0.5 * terms[j][0], 0.5 * terms[j][1])
        out.append((own[0] - 0.5 * terms[j + 2][0], own[1] - 0.5 * terms[j + 2][1]))
    for m in range(BLOCK, 0, -1):
        for j in range(BLOCK + m - 2, BLOCK - m - 1, -2):
            out[j] = (out[j][0] - out[BLOCK + m][0], out[j][1] - out[BLOCK + m][1])
    return out


def swap_groups(a):
    group = lax.broadcasted_iota(jnp.int32, a[0].shape, 1) // 32
    upper = group >= 2
    odd = group % 2 == 1
    c0 = jnp.where(upper, pltpu.roll(a[2], 64, 1), a[0])
    c2 = jnp.where(upper, a[2], pltpu.roll(a[0], 64, 1))
    c1 = jnp.where(upper, pltpu.roll(a[3], 64, 1), a[1])
    c3 = jnp.where(upper, a[3], pltpu.roll(a[1], 64, 1))
    return (
        jnp.where(odd, pltpu.roll(c1, 32, 1), c0),
        jnp.where(odd, c1, pltpu.roll(c0, 96, 1)),
        jnp.where(odd, pltpu.roll(c3, 32, 1), c2),
        jnp.where(odd, c3, pltpu.roll(c2, 96, 1)),
    )


def tile_of(tm, sp):
    cx, cz, cy, core = tm // 4, tm % 4, sp // 2, sp % 2
    zhi = cz // 2
    zlo = (cz + 1) // 2 % 2
    a = cx + zlo * (7 - 2 * cx)
    b = cy + zhi * (7 - 2 * cy)
    return 2 * a + core, b


def device_of(xi, yi):
    a, core = xi // 2, xi % 2
    zlo, zhi = a // 4, yi // 4
    cx = a + zlo * (7 - 2 * a)
    cy = yi + zhi * (7 - 2 * yi)
    cz = zlo + zhi * (3 - 2 * zlo)
    return cx * 4 + cz, cy * 2 + core


def two_terms(a):
    head = a.astype(jnp.bfloat16)
    return head, (a - head.astype(F32)).astype(jnp.bfloat16)


def dot(a, head, rest):
    a_head, a_rest = two_terms(a)
    small = jnp.dot(a_rest, head, preferred_element_type=F32) + jnp.dot(a_head, rest, preferred_element_type=F32)
    return jnp.dot(a_head, head, preferred_element_type=F32) + small


def kernel(
    anum, cond, source_in, start_in, guess_in, classes_in, dft_in, back_in, trig_in, recv2,
    source, start, guess, classes, dft, back, dft0, dft1, back0, back1, trig, insem, send1, recv1, send2a, send2b, cls_send, cls_recv, kap, wxm, wxp, wym, wyp, wzi, wzm, wzp, wc,
    u0, u1, u2, u3, acc, beta, tsem, ksend, krecv, hsend, hrecv, selfsem,
):
    tm = lax.axis_index("tm")
    sp = lax.axis_index("space")
    me = tm * NSP + sp
    xi, yi = tile_of(tm, sp)
    tile = xi * 8 + yi

    planes = [[(tm // 4 + dx) % 4 * 4 + (tm + dz) % 4 for dz in range(4)] for dx in range(4)]
    places = [[(sp // 2 + dy) % 4 * 2 + (sp + dc) % 2 for dc in range(2)] for dy in range(4)]

    zhi = tm % 4 // 2
    half_lanes = pl.ds(pl.multiple_of(zhi * 128, 128), 128)
    pair_rows = pl.ds(pl.multiple_of(xi // 2 * 32, 32), 32)
    pairs = [
        (source_in, source),
        (classes_in.at[:, pair_rows, half_lanes], classes),
        (trig_in, trig),
        (dft_in, dft),
        (back_in, back),
    ]
    loads = [pltpu.make_async_copy(a, b, insem.at[i]) for i, (a, b) in enumerate(pairs)]
    firsts = [
        pltpu.make_async_copy(start_in, start, insem.at[5]),
        pltpu.make_async_copy(guess_in, guess, insem.at[6]),
    ]
    for copy in loads:
        copy.start()

    @pl.when(tm == 0)
    def _():
        for copy in firsts:
            copy.start()


    barrier = pltpu.get_barrier_semaphore()
    for dx, dz, dy, dc in OFFSETS:
        pl.semaphore_signal(barrier, inc=1, device_id=(planes[dx][dz], places[dy][dc]), device_id_type=MESH)

    low_x, high_x, low_y, high_y = xi > 0, xi < 15, yi > 0, yi < 7
    beside = {-1: low_x, 1: high_x}, {-1: low_y, 1: high_y}

    def here(dx, dy):
        if dx and dy:
            return jnp.logical_and(beside[0][dx], beside[1][dy])
        return beside[0][dx] if dx else beside[1][dy]

    def span(d, low, middle, high):
        return {-1: low, 0: middle, 1: high}[d]

    def halo(dx, dy):
        return (
            span(dx, pl.ds(0, DEPTH), pl.ds(DEPTH, 16), pl.ds(DEPTH + 16, DEPTH)),
            span(dy, pl.ds(36, 4), pl.ds(0, 32), pl.ds(32, 4)),
        )

    log_alpha = jnp.log(jnp.full((8, 128), anum[0].astype(F32) / 32.0, F32))
    alpha = anum[0].astype(F32) / 32.0
    n0 = (2 * tm).astype(F32)
    scales = [jnp.exp(log_alpha * (n0 + t) / STEPS) for t in range(2)]

    loads[0].wait()

    @pl.when(tm == 0)
    def _():
        for copy in firsts:
            copy.wait()

        def correct(x, carry):
            rows = pl.ds(pl.multiple_of(x * 16, 16), 16)
            for z in range(2):
                source[0, z, rows, :] = source[0, z, rows, :] + (start[z, rows, :] - alpha * guess[z, rows, :])
            return carry

        lax.fori_loop(0, 16, correct, 0)

    def pack(step, carry):
        todo = []
        for x, xt in [(4 * step + i, xt) for i in range(4) for xt in range(2)]:
            rows = pl.ds(pl.multiple_of(x * 16 + xt * 8, 8), 8)
            for h in range(2):
                lanes = slice(h * 128, h * 128 + 128)
                parts = []
                for t in range(2):
                    for z in range(2):
                        value = source[t, z, rows, lanes]
                        parts.append(value * scales[t])
                for j, value in enumerate(swap_groups(parts)):
                    at = pl.multiple_of((x * 8 + h * 4 + j) * 16 + xt * 8, 8)
                    todo.append((at, value))
        for at, value in todo:
            send1[pl.ds(at, 8), :] = value
        return carry

    lax.fori_loop(0, 4, pack, 0)

    loads[1].wait()
    for core in range(2):
        parts = [
            classes[z, core * 16 + xt * 8 : core * 16 + xt * 8 + 8, :]
            for xt in range(2)
            for z in range(2)
        ]
        for j, value in enumerate(swap_groups(parts)):
            cls_send[core, j] = value

    pl.semaphore_wait(barrier, NDEV - 1)

    def cls_go(k, carry):
        other = (sp + k) % NSP
        ocy, ocore = other // 2, other % 2
        j = ocy + zhi * (3 - 2 * ocy)
        pltpu.make_async_remote_copy(
            src_ref=cls_send.at[ocore, j],
            dst_ref=cls_recv.at[pl.ds(pl.multiple_of(sp * 8, 8), 8)],
            send_sem=tsem.at[4],
            recv_sem=tsem.at[5],
            device_id=(tm, other),
            device_id_type=MESH,
        ).start()
        return carry

    lax.fori_loop(1, NSP, cls_go, 0)

    def rows16(index):
        return pl.ds(pl.multiple_of(index * 16, 16), 16)

    tiles_x = [[tile_of(planes[dx][dz], sp)[0] - sp % 2 for dz in range(4)] for dx in range(4)]
    tiles_y = [[tile_of(planes[0][dz], places[dy][0])[1] for dz in range(4)] for dy in range(4)]
    for dx, dz, dy, dc in OFFSETS:
        other = (tiles_x[dx][dz] + (sp + dc) % 2) * 8 + tiles_y[dy][dz]
        pltpu.make_async_remote_copy(
            src_ref=send1.at[rows16(other)],
            dst_ref=recv1.at[rows16(me)],
            send_sem=tsem.at[0],
            recv_sem=tsem.at[1],
            device_id=(planes[dx][dz], places[dy][dc]),
            device_id_type=MESH,
        ).start()
    recv1[rows16(me), :] = send1[rows16(tile), :]
    mycy, mycore = sp // 2, sp % 2
    cls_recv[pl.ds(pl.multiple_of(sp * 8, 8), 8), :] = cls_send[mycore, mycy + zhi * (3 - 2 * mycy)]

    for copy in loads[2:]:
        copy.wait()
    dft0[...], dft1[...] = two_terms(dft[...])
    back0[...], back1[...] = two_terms(back[...])
    for j, (re, im) in enumerate(chebyshev_table(log_alpha, trig[0:8, :], trig[8:16, :])):
        beta[j, 0:1, :] = re[0:1]
        beta[j, 1:2, :] = im[0:1]
        beta[j, 2:3, :] = -im[0:1]
        beta[j, 3:4, :] = re[4:5]

    for dx, dy in SIDES:

        @pl.when(jnp.logical_not(here(dx, dy)))
        def _(dx=dx, dy=dy):
            xs, ys = halo(dx, dy)
            for ref in (kap, u0.at[0], u0.at[1], u3.at[0], u3.at[1]):
                ref[xs, :, ys, :] = jnp.zeros((xs.size, 2, ys.size, 128), F32)

    some = cls_recv.at[pl.ds(0, 56)]
    pltpu.make_async_copy(some, some, tsem.at[5]).wait()

    def conductivities(xx, carry):
        codes = cls_recv[pl.ds(xx, 8, stride=8), :]
        value = jnp.zeros((8, 128), F32)
        for level in range(8):
            value = jnp.where(codes == level, cond[level], value)
        full = jnp.concatenate([value] * 16, axis=0).T
        for xt in range(2):
            kap[DEPTH + xt * 8 + xx, :, 0:32, :] = full[xt * 64 : xt * 64 + 64].reshape(2, 32, 128)
        return carry

    lax.fori_loop(0, 8, conductivities, 0)

    def edge(dx, dy):
        return (
            span(dx, pl.ds(DEPTH, DEPTH), pl.ds(DEPTH, 16), pl.ds(16, DEPTH)),
            span(dy, pl.ds(0, 4), pl.ds(0, 32), pl.ds(28, 4)),
        )

    def exchange(ref, send, recv, act):
        for i, (dx, dy) in enumerate(SIDES):

            @pl.when(here(dx, dy))
            def _(i=i, dx=dx, dy=dy):
                xs, ys = edge(dx, dy)
                xd, yd = halo(-dx, -dy)
                back_at = SIDES.index((-dx, -dy))
                copy = pltpu.make_async_remote_copy(
                    src_ref=ref.at[xs, :, ys, :],
                    dst_ref=ref.at[xd, :, yd, :],
                    send_sem=send.at[i],
                    recv_sem=recv.at[back_at],
                    device_id=device_of(
                        jnp.clip(xi + dx, 0, 15) if dx else xi, jnp.clip(yi + dy, 0, 7) if dy else yi
                    ),
                    device_id_type=MESH,
                )
                if act == "start":
                    copy.start()
                else:
                    copy.wait_send()
                    xh, yh = halo(dx, dy)
                    got = ref.at[xh, :, yh, :]
                    pltpu.make_async_copy(got, got, recv.at[i]).wait()

    exchange(kap, ksend, krecv, "start")
    most = recv1.at[pl.ds(0, (NDEV - 1) * 16)]
    pltpu.make_async_copy(most, most, tsem.at[1]).wait()

    def forward(quad, carry):
        rows = []
        for i in range(4):
            cells = recv1[pl.ds(quad * 4 + i, 128, stride=16), :].T
            rows.append(jnp.concatenate([cells[:64], cells[64:]], axis=1))
        spectrum = dot(jnp.concatenate(rows, axis=0), dft0[...], dft1[...])
        for i in range(4):
            x = quad * 4 + i
            for z in range(2):
                at = i * 64 + z * 32
                re = spectrum[at : at + 32, 0:128]
                im = spectrum[at : at + 32, 128:256]
                u0[0, DEPTH + x, z, 0:32] = re
                u0[1, DEPTH + x, z, 0:32] = im
                acc[0, x, z] = beta[0, 0:1, :] * re + beta[0, 2:3, :] * im
                acc[1, x, z] = beta[0, 1:2, :] * re + beta[0, 3:4, :] * im
        return carry

    lax.fori_loop(0, 4, forward, 0)

    def swap(block, p, act):
        exchange((u0, u3)[block].at[p], hsend.at[block, p], hrecv.at[block, p], act)

    def chebyshev(block, p, half=None):
        begin = (u0, u3)[block]
        for m in range(BLOCK):
            now = (begin, u1, begin, u2)[m]
            old = (None, begin, u1, begin)[m]
            new = (u1, begin, u2, u3)[m]
            last = m == BLOCK - 1
            spare = BLOCK - 1 - m
            h = slice(0, 32 if last else 40)

            def sweep(first, count, now=now, old=old, new=new, last=last, h=h):
                field = [[now[p, first + i, z] for z in range(2)] for i in range(-1, count + 1)]
                values = []
                for i in range(count):
                    x = first + i
                    below, mid, above = field[i], field[i + 1], field[i + 2]
                    for z in range(2):
                        other = mid[1 - z][h]
                        outer = pltpu.roll(other, 1 if z == 0 else 127, 1)
                        before = pltpu.roll(mid[z], 1, 0)[h]
                        after = pltpu.roll(mid[z], 39, 0)[h]
                        value = wc[x, z, h] * mid[z][h] + wzi[x, h] * other
                        value = value + (wxm[x, z, h] * below[z][h] + wxp[x, z, h] * above[z][h])
                        if old is not None:
                            value = value - old[p, x, z, h]
                        rest = wym[x, z, h] * before + wyp[x, z, h] * after
                        value = value + (rest + (wzm if z == 0 else wzp)[x, h] * outer)
                        values.append((x, z, mid[z][h], value))
                if last:
                    totals = []
                    for x, z, own, value in values:
                        terms = [u1[p, x, z, h], old[p, x, z, h], own, value]
                        for to in range(2):
                            at = 2 * p + to
                            total = beta[BLOCK * block + 1, at : at + 1, :] * terms[0]
                            for i in range(1, 4):
                                total = total + beta[BLOCK * block + 1 + i, at : at + 1, :] * terms[i]
                            totals.append((to, x, z, acc[to, x - DEPTH, z] + total))
                    for to, x, z, total in totals:
                        acc[to, x - DEPTH, z] = total
                if not last or block == 0:
                    for x, z, own, value in values:
                        new[p, x, z, h] = value

            begin_at = DEPTH + 8 + spare if half == 1 else DEPTH - spare
            end_at = DEPTH + 8 + spare if half == 0 else DEPTH + 16 + spare
            steps, rest = divmod(end_at - begin_at, UNROLL)

            def several(step, carry, sweep=sweep, begin_at=begin_at):
                sweep(begin_at + step * UNROLL, UNROLL)
                return carry

            if steps > 1:
                lax.fori_loop(0, steps, several, 0)
            else:
                several(0, 0)
            if rest:
                sweep(begin_at + steps * UNROLL, rest)

    swap(0, 0, "start")
    swap(0, 1, "start")
    exchange(kap, ksend, krecv, "wait")

    row_at = lax.broadcasted_iota(jnp.int32, (40, 128), 0)
    pair_at = lax.broadcasted_iota(jnp.int32, (40, 128), 1) % 8
    one = jnp.ones((40, 128), F32)
    inside_low = jnp.where(low_y, 1.0, 0.0).astype(F32)
    inside_high = jnp.where(high_y, 1.0, 0.0).astype(F32)
    columns = jnp.where(row_at < 32, one, jnp.where(row_at < 36, one * inside_high, one * inside_low)) * (1.0 / 12.0)

    def weights(x, carry):
        total = [None, None]
        inside_x = jnp.logical_and(jnp.logical_or(x >= DEPTH, low_x), jnp.logical_or(x < DEPTH + 16, high_x))
        part = columns * jnp.where(inside_x, 1.0, 0.0).astype(F32)
        k = [kap[x, z] for z in range(2)]
        for z in range(2):
            low = (k[z] + kap[x - 1, z]) * part
            high = (k[z] + kap[x + 1, z]) * part
            wxm[x, z] = low
            wxp[x, z] = high
            before = (k[z] + pltpu.roll(k[z], 1, 0)) * part
            after = (k[z] + pltpu.roll(k[z], 39, 0)) * part
            wym[x, z] = before
            wyp[x, z] = after
            total[z] = (low + high) + (before + after)
        inside = (k[0] + k[1]) * part
        below = (k[0] + jnp.where(pair_at == 0, 0.0, pltpu.roll(k[1], 1, 1))) * part
        above = (k[1] + jnp.where(pair_at == 7, 0.0, pltpu.roll(k[0], 127, 1))) * part
        wzi[x] = inside
        wzm[x] = jnp.where(pair_at == 0, 0.0, below)
        wzp[x] = jnp.where(pair_at == 7, 0.0, above)
        wc[x, 0] = part * 24.0 - (total[0] + (inside + below))
        wc[x, 1] = part * 24.0 - (total[1] + (inside + above))
        return carry

    lax.fori_loop(1, 23, weights, 0)

    for p in range(2):
        swap(0, p, "wait")
        chebyshev(0, p)
        swap(1, p, "start")

    def inverse(quad):
        rows = []
        for i in range(4):
            x = quad * 4 + i
            rows.append(
                jnp.concatenate([acc[0, x].reshape(64, 128), acc[1, x].reshape(64, 128)], axis=1)
            )
        times = dot(jnp.concatenate(rows, axis=0), back0[...], back1[...])
        half_out = send2a if quad < 2 else send2b
        for i in range(4):
            own = times[i * 64 : i * 64 + 64]
            cells = jnp.concatenate([own[:, :128], own[:, 128:]], axis=0)
            half_out[pl.ds(quad % 2 * 4 + i, 128, stride=8), :] = cells.T

    kept = []
    for half, half_out in enumerate((send2a, send2b)):
        for p in range(2):
            if half == 0:
                swap(1, p, "wait")
            chebyshev(1, p, half)
        inverse(2 * half)
        inverse(2 * half + 1)
        mine = pl.ds(pl.multiple_of(tile * 16 + half * 8, 8), 8)
        for dx, dz, dy, dc in OFFSETS:
            to = planes[dx][dz] * NSP + places[dy][dc]
            pltpu.make_async_remote_copy(
                src_ref=half_out.at[pl.ds(pl.multiple_of(to * 8, 8), 8)],
                dst_ref=recv2.at[mine],
                send_sem=tsem.at[2],
                recv_sem=tsem.at[3],
                device_id=(planes[dx][dz], places[dy][dc]),
                device_id_type=MESH,
            ).start()
        stays = pltpu.make_async_copy(half_out.at[pl.ds(pl.multiple_of(me * 8, 8), 8)], recv2.at[mine], selfsem.at[half])
        stays.start()
        kept.append(stays)
    most2 = recv2.at[pl.ds(0, (NDEV - 1) * 16)]
    for stays in kept:
        stays.wait()
    pltpu.make_async_copy(most2, most2, tsem.at[3]).wait()

    pltpu.make_async_copy(most, most, tsem.at[0]).wait()
    pltpu.make_async_copy(most2, most2, tsem.at[2]).wait()
    pltpu.make_async_copy(some, some, tsem.at[4]).wait()


def unpack_kernel(anum, tiles, out):
    log_alpha = jnp.log(jnp.full((8, 128), anum[0].astype(F32) / 32.0, F32))
    n0 = (2 * lax.axis_index("tm")).astype(F32)
    unscales = [jnp.exp(-log_alpha * (n0 + t) / STEPS) for t in range(2)]

    def pair(step, carry):
        todo = []
        for x, xt in [(2 * step + i, xt) for i in range(2) for xt in range(2)]:
            row = pl.multiple_of(x * 16 + xt * 8, 8)
            for h in range(2):
                parts = [
                    tiles[pl.ds(pl.multiple_of((x * 8 + h * 4 + j) * 16 + xt * 8, 8), 8), :] for j in range(4)
                ]
                for i, value in enumerate(swap_groups(parts)):
                    todo.append((i // 2, i % 2, row, h * 128, value * unscales[i // 2]))
        for t, z, row, lane, value in todo:
            out[t, z, pl.ds(row, 8), lane : lane + 128] = value
        return carry

    lax.fori_loop(0, out.shape[2] // 32, pair, 0)


def body(source, start_field, last_guess, classes, conductivity, alpha_num):
    consts = [jnp.asarray(t) for t in tables()]
    smem = pl.BlockSpec(memory_space=pltpu.SMEM)
    hbm = pl.BlockSpec(memory_space=pltpu.HBM)
    BF16 = jnp.bfloat16
    V = pltpu.VMEM
    tiles = pl.pallas_call(
        kernel,
        out_shape=jax.ShapeDtypeStruct((2048, 128), F32),
        in_specs=[smem, smem] + [hbm] * 7,
        out_specs=hbm,
        scratch_shapes=[
            V((2, 2, 256, 256), F32), V((2, 256, 256), F32), V((2, 256, 256), F32), V((2, 32, 128), jnp.int32),
            V((256, 256), F32), V((256, 256), F32), V((256, 256), BF16), V((256, 256), BF16), V((256, 256), BF16), V((256, 256), BF16), V((16, 128), F32),
            pltpu.SemaphoreType.DMA((7,)),
            V((2048, 128), F32), V((2048, 128), F32), V((1024, 128), F32), V((1024, 128), F32),
            V((2, 4, 8, 128), jnp.int32), V((64, 128), jnp.int32),
            V((24, 2, 40, 128), F32), V((24, 2, 40, 128), F32), V((24, 2, 40, 128), F32), V((24, 2, 40, 128), F32),
            V((24, 2, 40, 128), F32),
            V((24, 40, 128), F32), V((24, 40, 128), F32), V((24, 40, 128), F32), V((24, 2, 40, 128), F32),
            V((2, 24, 2, 40, 128), F32), V((2, 24, 2, 40, 128), F32), V((2, 24, 2, 40, 128), F32), V((2, 24, 2, 40, 128), F32), V((2, 16, 2, 32, 128), F32), V((CHEB + 1, 8, 128), F32),
            pltpu.SemaphoreType.DMA((6,)),
            pltpu.SemaphoreType.DMA((8,)), pltpu.SemaphoreType.DMA((8,)),
            pltpu.SemaphoreType.DMA((2, 2, 8)), pltpu.SemaphoreType.DMA((2, 2, 8)), pltpu.SemaphoreType.DMA((2,)),
        ],
        compiler_params=pltpu.CompilerParams(
            collective_id=1, has_side_effects=True, vmem_limit_bytes=62 * 2**20
        ),
    )(alpha_num, conductivity, source, start_field, last_guess, classes, *consts)
    steps = 2
    return pl.pallas_call(
        unpack_kernel,
        grid=(steps,),
        out_shape=jax.ShapeDtypeStruct((2, 2, 256, 256), F32),
        in_specs=[smem, pl.BlockSpec((2048 // steps, 128), lambda i: (i, 0))],
        out_specs=pl.BlockSpec((2, 2, 256 // steps, 256), lambda i: (0, 0, i, 0)),
    )(alpha_num, tiles)


def solution(mesh):
    placed = (
        P("tm", "space", None, None),
        P("space", None, None),
        P("space", None, None),
        P("space", None, None),
        P(),
        P(),
    )
    return jax.shard_map(
        body, mesh=mesh, in_specs=placed, out_specs=P("tm", "space", None, None), check_vma=False
    )
```

```python
import functools

import jax
import jax.numpy as jnp
import numpy as np
from jax import lax
from jax.experimental import pallas as pl
from jax.experimental.pallas import tpu as pltpu
from jax.sharding import PartitionSpec as P

MESH = pl.DeviceIdType.MESH
F32 = jnp.float32
CHEB = 8
STEPS = 32
HALF_SPAN = 12.0
NTM, NSP = 16, 8
NDEV = NTM * NSP
OFFSETS = sorted(
    [(dx, dz, dy, dc) for dx in range(4) for dz in range(4) for dy in range(4) for dc in range(2)][1:],
    key=lambda o: -sum(min(d, 4 - d) for d in o[:3]),
)
DEPTH = 4
BLOCK = 4
UNROLL = 8
SIDES = [(-1, 0), (1, 0), (0, -1), (0, 1), (-1, -1), (-1, 1), (1, -1), (1, 1)]


def tables():
    lane = np.arange(128)
    slot, pair = lane // 8, lane % 8
    dft = np.zeros((2, 128, 2, 128))
    back = np.zeros((2, 128, 2, 128))
    same = (pair[:, None] == pair[None, :]).astype(np.float64)
    for half in range(2):
        n = 2 * slot + half
        angle = 2 * np.pi * ((n[:, None] * slot[None, :]) % STEPS) / STEPS
        sign = np.where(n % 2 == 0, 1.0, -1.0)[:, None]
        first = (slot == 0)[None, :]
        real = np.cos(angle)
        imag = np.where(first, sign, -np.sin(angle))
        weight = np.where(first, 1.0, 2.0) / STEPS
        dft[half, :, 0, :] = same * real
        dft[half, :, 1, :] = same * imag
        back[0, :, half, :] = (same * real * weight).T
        back[1, :, half, :] = (same * imag * weight).T
    trig = np.zeros((16, 128))
    for row in range(8):
        freq = np.where((slot == 0) & (row >= 4), 16, slot)
        angle = 2 * np.pi * freq / STEPS
        trig[row] = np.cos(angle)
        trig[8 + row] = np.where(slot == 0, 0.0, np.sin(angle))
    return (
        dft.reshape(256, 256).astype(np.float32),
        back.reshape(256, 256).astype(np.float32),
        trig.astype(np.float32),
    )


def cmul(a, b):
    return (a[0] * b[0] - a[1] * b[1], a[0] * b[1] + a[1] * b[0])


def cinv(a):
    denom = a[0] * a[0] + a[1] * a[1]
    return (a[0] / denom, -a[1] / denom)


def chebyshev_table(log_alpha, cos_f, sin_f):
    ratio = jnp.exp(log_alpha / STEPS)
    center = (1.0 - ratio * cos_f + HALF_SPAN, ratio * sin_f)
    sigma = (center[0] / HALF_SPAN, center[1] / HALF_SPAN)
    rho = [cinv(sigma)]
    for _ in range(CHEB):
        rho.append(cinv((2.0 * sigma[0] - rho[-1][0], 2.0 * sigma[1] - rho[-1][1])))
    inner = (jnp.ones_like(cos_f), jnp.zeros_like(cos_f))
    gains = [None] * (CHEB + 1)
    for j in range(CHEB, -1, -1):
        if j < CHEB:
            step = cmul(cmul(rho[j + 1], rho[j]), inner)
            inner = (1.0 + step[0], step[1])
        scale = cinv(center) if j == 0 else (rho[j][0] / 6.0, rho[j][1] / 6.0)
        gains[j] = cmul(scale, inner)
    level = (jnp.ones_like(cos_f), jnp.zeros_like(cos_f))
    terms = []
    for j in range(CHEB + 1):
        terms.append(cmul(gains[j], level))
        level = cmul(level, rho[j])
    zero = (jnp.zeros_like(cos_f), jnp.zeros_like(cos_f))
    terms += [zero, zero]
    out = []
    for j in range(CHEB + 1):
        own = terms[j] if j == 0 else (0.5 * terms[j][0], 0.5 * terms[j][1])
        out.append((own[0] - 0.5 * terms[j + 2][0], own[1] - 0.5 * terms[j + 2][1]))
    for m in range(BLOCK, 0, -1):
        for j in range(BLOCK + m - 2, BLOCK - m - 1, -2):
            out[j] = (out[j][0] - out[BLOCK + m][0], out[j][1] - out[BLOCK + m][1])
    return out


def swap_groups(a):
    group = lax.broadcasted_iota(jnp.int32, a[0].shape, 1) // 32
    upper = group >= 2
    odd = group % 2 == 1
    c0 = jnp.where(upper, pltpu.roll(a[2], 64, 1), a[0])
    c2 = jnp.where(upper, a[2], pltpu.roll(a[0], 64, 1))
    c1 = jnp.where(upper, pltpu.roll(a[3], 64, 1), a[1])
    c3 = jnp.where(upper, a[3], pltpu.roll(a[1], 64, 1))
    return (
        jnp.where(odd, pltpu.roll(c1, 32, 1), c0),
        jnp.where(odd, c1, pltpu.roll(c0, 96, 1)),
        jnp.where(odd, pltpu.roll(c3, 32, 1), c2),
        jnp.where(odd, c3, pltpu.roll(c2, 96, 1)),
    )


def tile_of(tm, sp):
    cx, cz, cy, core = tm // 4, tm % 4, sp // 2, sp % 2
    zhi = cz // 2
    zlo = (cz + 1) // 2 % 2
    a = cx + zlo * (7 - 2 * cx)
    b = cy + zhi * (7 - 2 * cy)
    return 2 * a + core, b


def device_of(xi, yi):
    a, core = xi // 2, xi % 2
    zlo, zhi = a // 4, yi // 4
    cx = a + zlo * (7 - 2 * a)
    cy = yi + zhi * (7 - 2 * yi)
    cz = zlo + zhi * (3 - 2 * zlo)
    return cx * 4 + cz, cy * 2 + core


def two_terms(a):
    head = a.astype(jnp.bfloat16)
    return head, (a - head.astype(F32)).astype(jnp.bfloat16)


def dot(a, head, rest):
    a_head, a_rest = two_terms(a)
    small = jnp.dot(a_rest, head, preferred_element_type=F32) + jnp.dot(a_head, rest, preferred_element_type=F32)
    return jnp.dot(a_head, head, preferred_element_type=F32) + small


def kernel(
    anum, cond, source_in, start_in, guess_in, classes_in, dft_in, back_in, trig_in, recv2,
    source, start, guess, classes, dft, back, dft0, dft1, back0, back1, trig, insem, send1, recv1, send2a, send2b, cls_send, cls_recv, kap, wxm, wxp, wym, wyp, wzi, wzm, wzp, wc,
    u0, u1, u2, u3, acc, beta, tsem, ksend, krecv, hsend, hrecv, selfsem,
):
    tm = lax.axis_index("tm")
    sp = lax.axis_index("space")
    me = tm * NSP + sp
    xi, yi = tile_of(tm, sp)
    tile = xi * 8 + yi

    planes = [[(tm // 4 + dx) % 4 * 4 + (tm + dz) % 4 for dz in range(4)] for dx in range(4)]
    places = [[(sp // 2 + dy) % 4 * 2 + (sp + dc) % 2 for dc in range(2)] for dy in range(4)]

    zhi = tm % 4 // 2
    half_lanes = pl.ds(pl.multiple_of(zhi * 128, 128), 128)
    pair_rows = pl.ds(pl.multiple_of(xi // 2 * 32, 32), 32)
    pairs = [
        (source_in, source),
        (classes_in.at[:, pair_rows, half_lanes], classes),
        (trig_in, trig),
        (dft_in, dft),
        (back_in, back),
    ]
    loads = [pltpu.make_async_copy(a, b, insem.at[i]) for i, (a, b) in enumerate(pairs)]
    firsts = [
        pltpu.make_async_copy(start_in, start, insem.at[5]),
        pltpu.make_async_copy(guess_in, guess, insem.at[6]),
    ]
    for copy in loads:
        copy.start()

    @pl.when(tm == 0)
    def _():
        for copy in firsts:
            copy.start()


    barrier = pltpu.get_barrier_semaphore()
    for dx, dz, dy, dc in OFFSETS:
        pl.semaphore_signal(barrier, inc=1, device_id=(planes[dx][dz], places[dy][dc]), device_id_type=MESH)

    low_x, high_x, low_y, high_y = xi > 0, xi < 15, yi > 0, yi < 7
    beside = {-1: low_x, 1: high_x}, {-1: low_y, 1: high_y}

    def here(dx, dy):
        if dx and dy:
            return jnp.logical_and(beside[0][dx], beside[1][dy])
        return beside[0][dx] if dx else beside[1][dy]

    def span(d, low, middle, high):
        return {-1: low, 0: middle, 1: high}[d]

    def halo(dx, dy):
        return (
            span(dx, pl.ds(0, DEPTH), pl.ds(DEPTH, 16), pl.ds(DEPTH + 16, DEPTH)),
            span(dy, pl.ds(36, 4), pl.ds(0, 32), pl.ds(32, 4)),
        )

    log_alpha = jnp.log(jnp.full((8, 128), anum[0].astype(F32) / 32.0, F32))
    alpha = anum[0].astype(F32) / 32.0
    n0 = (2 * tm).astype(F32)
    scales = [jnp.exp(log_alpha * (n0 + t) / STEPS) for t in range(2)]

    loads[0].wait()

    @pl.when(tm == 0)
    def _():
        for copy in firsts:
            copy.wait()

        def correct(x, carry):
            rows = pl.ds(pl.multiple_of(x * 16, 16), 16)
            for z in range(2):
                source[0, z, rows, :] = source[0, z, rows, :] + (start[z, rows, :] - alpha * guess[z, rows, :])
            return carry

        lax.fori_loop(0, 16, correct, 0)

    def pack(step, carry):
        todo = []
        for x, xt in [(4 * step + i, xt) for i in range(4) for xt in range(2)]:
            rows = pl.ds(pl.multiple_of(x * 16 + xt * 8, 8), 8)
            for h in range(2):
                lanes = slice(h * 128, h * 128 + 128)
                parts = []
                for t in range(2):
                    for z in range(2):
                        value = source[t, z, rows, lanes]
                        parts.append(value * scales[t])
                for j, value in enumerate(swap_groups(parts)):
                    at = pl.multiple_of((x * 8 + h * 4 + j) * 16 + xt * 8, 8)
                    todo.append((at, value))
        for at, value in todo:
            send1[pl.ds(at, 8), :] = value
        return carry

    lax.fori_loop(0, 4, pack, 0)

    loads[1].wait()
    for core in range(2):
        parts = [
            classes[z, core * 16 + xt * 8 : core * 16 + xt * 8 + 8, :]
            for xt in range(2)
            for z in range(2)
        ]
        for j, value in enumerate(swap_groups(parts)):
            cls_send[core, j] = value

    pl.semaphore_wait(barrier, NDEV - 1)

    def cls_go(k, carry):
        other = (sp + k) % NSP
        ocy, ocore = other // 2, other % 2
        j = ocy + zhi * (3 - 2 * ocy)
        pltpu.make_async_remote_copy(
            src_ref=cls_send.at[ocore, j],
            dst_ref=cls_recv.at[pl.ds(pl.multiple_of(sp * 8, 8), 8)],
            send_sem=tsem.at[4],
            recv_sem=tsem.at[5],
            device_id=(tm, other),
            device_id_type=MESH,
        ).start()
        return carry

    lax.fori_loop(1, NSP, cls_go, 0)

    def rows16(index):
        return pl.ds(pl.multiple_of(index * 16, 16), 16)

    tiles_x = [[tile_of(planes[dx][dz], sp)[0] - sp % 2 for dz in range(4)] for dx in range(4)]
    tiles_y = [[tile_of(planes[0][dz], places[dy][0])[1] for dz in range(4)] for dy in range(4)]
    for dx, dz, dy, dc in OFFSETS:
        other = (tiles_x[dx][dz] + (sp + dc) % 2) * 8 + tiles_y[dy][dz]
        pltpu.make_async_remote_copy(
            src_ref=send1.at[rows16(other)],
            dst_ref=recv1.at[rows16(me)],
            send_sem=tsem.at[0],
            recv_sem=tsem.at[1],
            device_id=(planes[dx][dz], places[dy][dc]),
            device_id_type=MESH,
        ).start()
    recv1[rows16(me), :] = send1[rows16(tile), :]
    mycy, mycore = sp // 2, sp % 2
    cls_recv[pl.ds(pl.multiple_of(sp * 8, 8), 8), :] = cls_send[mycore, mycy + zhi * (3 - 2 * mycy)]

    for copy in loads[2:]:
        copy.wait()
    dft0[...], dft1[...] = two_terms(dft[...])
    back0[...], back1[...] = two_terms(back[...])
    for j, (re, im) in enumerate(chebyshev_table(log_alpha, trig[0:8, :], trig[8:16, :])):
        beta[j, 0:1, :] = re[0:1]
        beta[j, 1:2, :] = im[0:1]
        beta[j, 2:3, :] = -im[0:1]
        beta[j, 3:4, :] = re[4:5]

    for dx, dy in SIDES:

        @pl.when(jnp.logical_not(here(dx, dy)))
        def _(dx=dx, dy=dy):
            xs, ys = halo(dx, dy)
            for ref in (kap, u0.at[0], u0.at[1], u3.at[0], u3.at[1]):
                ref[xs, :, ys, :] = jnp.zeros((xs.size, 2, ys.size, 128), F32)

    some = cls_recv.at[pl.ds(0, 56)]
    pltpu.make_async_copy(some, some, tsem.at[5]).wait()

    def conductivities(xx, carry):
        codes = cls_recv[pl.ds(xx, 8, stride=8), :]
        value = jnp.zeros((8, 128), F32)
        for level in range(8):
            value = jnp.where(codes == level, cond[level], value)
        full = jnp.concatenate([value] * 16, axis=0).T
        for xt in range(2):
            kap[DEPTH + xt * 8 + xx, :, 0:32, :] = full[xt * 64 : xt * 64 + 64].reshape(2, 32, 128)
        return carry

    lax.fori_loop(0, 8, conductivities, 0)

    def edge(dx, dy):
        return (
            span(dx, pl.ds(DEPTH, DEPTH), pl.ds(DEPTH, 16), pl.ds(16, DEPTH)),
            span(dy, pl.ds(0, 4), pl.ds(0, 32), pl.ds(28, 4)),
        )

    def exchange(ref, send, recv, act):
        for i, (dx, dy) in enumerate(SIDES):

            @pl.when(here(dx, dy))
            def _(i=i, dx=dx, dy=dy):
                xs, ys = edge(dx, dy)
                xd, yd = halo(-dx, -dy)
                back_at = SIDES.index((-dx, -dy))
                copy = pltpu.make_async_remote_copy(
                    src_ref=ref.at[xs, :, ys, :],
                    dst_ref=ref.at[xd, :, yd, :],
                    send_sem=send.at[i],
                    recv_sem=recv.at[back_at],
                    device_id=device_of(
                        jnp.clip(xi + dx, 0, 15) if dx else xi, jnp.clip(yi + dy, 0, 7) if dy else yi
                    ),
                    device_id_type=MESH,
                )
                if act == "start":
                    copy.start()
                else:
                    copy.wait_send()
                    xh, yh = halo(dx, dy)
                    got = ref.at[xh, :, yh, :]
                    pltpu.make_async_copy(got, got, recv.at[i]).wait()

    exchange(kap, ksend, krecv, "start")
    most = recv1.at[pl.ds(0, (NDEV - 1) * 16)]
    pltpu.make_async_copy(most, most, tsem.at[1]).wait()

    def forward(quad, carry):
        rows = []
        for i in range(4):
            cells = recv1[pl.ds(quad * 4 + i, 128, stride=16), :].T
            rows.append(jnp.concatenate([cells[:64], cells[64:]], axis=1))
        spectrum = dot(jnp.concatenate(rows, axis=0), dft0[...], dft1[...])
        for i in range(4):
            x = quad * 4 + i
            for z in range(2):
                at = i * 64 + z * 32
                re = spectrum[at : at + 32, 0:128]
                im = spectrum[at : at + 32, 128:256]
                u0[0, DEPTH + x, z, 0:32] = re
                u0[1, DEPTH + x, z, 0:32] = im
                acc[0, x, z] = beta[0, 0:1, :] * re + beta[0, 2:3, :] * im
                acc[1, x, z] = beta[0, 1:2, :] * re + beta[0, 3:4, :] * im
        return carry

    lax.fori_loop(0, 4, forward, 0)

    def swap(block, p, act):
        exchange((u0, u3)[block].at[p], hsend.at[block, p], hrecv.at[block, p], act)

    def chebyshev(block, p, half=None):
        begin = (u0, u3)[block]
        for m in range(BLOCK):
            now = (begin, u1, begin, u2)[m]
            old = (None, begin, u1, begin)[m]
            new = (u1, begin, u2, u3)[m]
            last = m == BLOCK - 1
            spare = BLOCK - 1 - m
            h = slice(0, 32 if last else 40)

            def sweep(first, count, now=now, old=old, new=new, last=last, h=h):
                field = [[now[p, first + i, z] for z in range(2)] for i in range(-1, count + 1)]
                values = []
                for i in range(count):
                    x = first + i
                    below, mid, above = field[i], field[i + 1], field[i + 2]
                    for z in range(2):
                        other = mid[1 - z][h]
                        outer = pltpu.roll(other, 1 if z == 0 else 127, 1)
                        before = pltpu.roll(mid[z], 1, 0)[h]
                        after = pltpu.roll(mid[z], 39, 0)[h]
                        value = wc[x, z, h] * mid[z][h] + wzi[x, h] * other
                        value = value + (wxm[x, z, h] * below[z][h] + wxp[x, z, h] * above[z][h])
                        if old is not None:
                            value = value - old[p, x, z, h]
                        rest = wym[x, z, h] * before + wyp[x, z, h] * after
                        value = value + (rest + (wzm if z == 0 else wzp)[x, h] * outer)
                        values.append((x, z, mid[z][h], value))
                if last:
                    totals = []
                    for x, z, own, value in values:
                        terms = [u1[p, x, z, h], old[p, x, z, h], own, value]
                        for to in range(2):
                            at = 2 * p + to
                            total = beta[BLOCK * block + 1, at : at + 1, :] * terms[0]
                            for i in range(1, 4):
                                total = total + beta[BLOCK * block + 1 + i, at : at + 1, :] * terms[i]
                            totals.append((to, x, z, acc[to, x - DEPTH, z] + total))
                    for to, x, z, total in totals:
                        acc[to, x - DEPTH, z] = total
                if not last or block == 0:
                    for x, z, own, value in values:
                        new[p, x, z, h] = value

            begin_at = DEPTH + 8 + spare if half == 1 else DEPTH - spare
            end_at = DEPTH + 8 + spare if half == 0 else DEPTH + 16 + spare
            steps, rest = divmod(end_at - begin_at, UNROLL)

            def several(step, carry, sweep=sweep, begin_at=begin_at):
                sweep(begin_at + step * UNROLL, UNROLL)
                return carry

            if steps > 1:
                lax.fori_loop(0, steps, several, 0)
            else:
                several(0, 0)
            if rest:
                sweep(begin_at + steps * UNROLL, rest)

    swap(0, 0, "start")
    exchange(kap, ksend, krecv, "wait")

    row_at = lax.broadcasted_iota(jnp.int32, (40, 128), 0)
    pair_at = lax.broadcasted_iota(jnp.int32, (40, 128), 1) % 8
    one = jnp.ones((40, 128), F32)
    inside_low = jnp.where(low_y, 1.0, 0.0).astype(F32)
    inside_high = jnp.where(high_y, 1.0, 0.0).astype(F32)
    columns = jnp.where(row_at < 32, one, jnp.where(row_at < 36, one * inside_high, one * inside_low)) * (1.0 / 12.0)

    def weights(x, carry):
        total = [None, None]
        inside_x = jnp.logical_and(jnp.logical_or(x >= DEPTH, low_x), jnp.logical_or(x < DEPTH + 16, high_x))
        part = columns * jnp.where(inside_x, 1.0, 0.0).astype(F32)
        k = [kap[x, z] for z in range(2)]
        for z in range(2):
            low = (k[z] + kap[x - 1, z]) * part
            high = (k[z] + kap[x + 1, z]) * part
            wxm[x, z] = low
            wxp[x, z] = high
            before = (k[z] + pltpu.roll(k[z], 1, 0)) * part
            after = (k[z] + pltpu.roll(k[z], 39, 0)) * part
            wym[x, z] = before
            wyp[x, z] = after
            total[z] = (low + high) + (before + after)
        inside = (k[0] + k[1]) * part
        below = (k[0] + jnp.where(pair_at == 0, 0.0, pltpu.roll(k[1], 1, 1))) * part
        above = (k[1] + jnp.where(pair_at == 7, 0.0, pltpu.roll(k[0], 127, 1))) * part
        wzi[x] = inside
        wzm[x] = jnp.where(pair_at == 0, 0.0, below)
        wzp[x] = jnp.where(pair_at == 7, 0.0, above)
        wc[x, 0] = part * 24.0 - (total[0] + (inside + below))
        wc[x, 1] = part * 24.0 - (total[1] + (inside + above))
        return carry

    lax.fori_loop(1, 23, weights, 0)
    swap(0, 1, "start")

    for p in range(2):
        swap(0, p, "wait")
        chebyshev(0, p)
        swap(1, p, "start")

    def inverse(quad):
        rows = []
        for i in range(4):
            x = quad * 4 + i
            rows.append(
                jnp.concatenate([acc[0, x].reshape(64, 128), acc[1, x].reshape(64, 128)], axis=1)
            )
        times = dot(jnp.concatenate(rows, axis=0), back0[...], back1[...])
        half_out = send2a if quad < 2 else send2b
        for i in range(4):
            own = times[i * 64 : i * 64 + 64]
            cells = jnp.concatenate([own[:, :128], own[:, 128:]], axis=0)
            half_out[pl.ds(quad % 2 * 4 + i, 128, stride=8), :] = cells.T

    kept = []
    for half, half_out in enumerate((send2a, send2b)):
        for p in range(2):
            if half == 0:
                swap(1, p, "wait")
            chebyshev(1, p, half)
        inverse(2 * half)
        inverse(2 * half + 1)
        mine = pl.ds(pl.multiple_of(tile * 16 + half * 8, 8), 8)
        for dx, dz, dy, dc in OFFSETS:
            to = planes[dx][dz] * NSP + places[dy][dc]
            pltpu.make_async_remote_copy(
                src_ref=half_out.at[pl.ds(pl.multiple_of(to * 8, 8), 8)],
                dst_ref=recv2.at[mine],
                send_sem=tsem.at[2],
                recv_sem=tsem.at[3],
                device_id=(planes[dx][dz], places[dy][dc]),
                device_id_type=MESH,
            ).start()
        stays = pltpu.make_async_copy(half_out.at[pl.ds(pl.multiple_of(me * 8, 8), 8)], recv2.at[mine], selfsem.at[half])
        stays.start()
        kept.append(stays)
    most2 = recv2.at[pl.ds(0, (NDEV - 1) * 16)]
    for stays in kept:
        stays.wait()
    pltpu.make_async_copy(most2, most2, tsem.at[3]).wait()

    pltpu.make_async_copy(most, most, tsem.at[0]).wait()
    pltpu.make_async_copy(most2, most2, tsem.at[2]).wait()
    pltpu.make_async_copy(some, some, tsem.at[4]).wait()


def unpack_kernel(anum, tiles, out):
    log_alpha = jnp.log(jnp.full((8, 128), anum[0].astype(F32) / 32.0, F32))
    n0 = (2 * lax.axis_index("tm")).astype(F32)
    unscales = [jnp.exp(-log_alpha * (n0 + t) / STEPS) for t in range(2)]

    def pair(step, carry):
        todo = []
        for x, xt in [(4 * step + i, xt) for i in range(4) for xt in range(2)]:
            row = pl.multiple_of(x * 16 + xt * 8, 8)
            for h in range(2):
                parts = [
                    tiles[pl.ds(pl.multiple_of((x * 8 + h * 4 + j) * 16 + xt * 8, 8), 8), :] for j in range(4)
                ]
                for i, value in enumerate(swap_groups(parts)):
                    todo.append((i // 2, i % 2, row, h * 128, value * unscales[i // 2]))
        for t, z, row, lane, value in todo:
            out[t, z, pl.ds(row, 8), lane : lane + 128] = value
        return carry

    lax.fori_loop(0, out.shape[2] // 64, pair, 0)


def body(source, start_field, last_guess, classes, conductivity, alpha_num):
    consts = [jnp.asarray(t) for t in tables()]
    smem = pl.BlockSpec(memory_space=pltpu.SMEM)
    hbm = pl.BlockSpec(memory_space=pltpu.HBM)
    BF16 = jnp.bfloat16
    V = pltpu.VMEM
    tiles = pl.pallas_call(
        kernel,
        out_shape=jax.ShapeDtypeStruct((2048, 128), F32),
        in_specs=[smem, smem] + [hbm] * 7,
        out_specs=hbm,
        scratch_shapes=[
            V((2, 2, 256, 256), F32), V((2, 256, 256), F32), V((2, 256, 256), F32), V((2, 32, 128), jnp.int32),
            V((256, 256), F32), V((256, 256), F32), V((256, 256), BF16), V((256, 256), BF16), V((256, 256), BF16), V((256, 256), BF16), V((16, 128), F32),
            pltpu.SemaphoreType.DMA((7,)),
            V((2048, 128), F32), V((2048, 128), F32), V((1024, 128), F32), V((1024, 128), F32),
            V((2, 4, 8, 128), jnp.int32), V((64, 128), jnp.int32),
            V((24, 2, 40, 128), F32), V((24, 2, 40, 128), F32), V((24, 2, 40, 128), F32), V((24, 2, 40, 128), F32),
            V((24, 2, 40, 128), F32),
            V((24, 40, 128), F32), V((24, 40, 128), F32), V((24, 40, 128), F32), V((24, 2, 40, 128), F32),
            V((2, 24, 2, 40, 128), F32), V((2, 24, 2, 40, 128), F32), V((2, 24, 2, 40, 128), F32), V((2, 24, 2, 40, 128), F32), V((2, 16, 2, 32, 128), F32), V((CHEB + 1, 8, 128), F32),
            pltpu.SemaphoreType.DMA((6,)),
            pltpu.SemaphoreType.DMA((8,)), pltpu.SemaphoreType.DMA((8,)),
            pltpu.SemaphoreType.DMA((2, 2, 8)), pltpu.SemaphoreType.DMA((2, 2, 8)), pltpu.SemaphoreType.DMA((2,)),
        ],
        compiler_params=pltpu.CompilerParams(
            collective_id=1, has_side_effects=True, vmem_limit_bytes=62 * 2**20
        ),
    )(alpha_num, conductivity, source, start_field, last_guess, classes, *consts)
    steps = 2
    return pl.pallas_call(
        unpack_kernel,
        grid=(steps,),
        out_shape=jax.ShapeDtypeStruct((2, 2, 256, 256), F32),
        in_specs=[smem, pl.BlockSpec((2048 // steps, 128), lambda i: (i, 0))],
        out_specs=pl.BlockSpec((2, 2, 256 // steps, 256), lambda i: (0, 0, i, 0)),
    )(alpha_num, tiles)


def solution(mesh):
    placed = (
        P("tm", "space", None, None),
        P("space", None, None),
        P("space", None, None),
        P("space", None, None),
        P(),
        P(),
    )
    return jax.shard_map(
        body, mesh=mesh, in_specs=placed, out_specs=P("tm", "space", None, None), check_vma=False
    )
```

```python
import functools

import jax
import jax.numpy as jnp
import numpy as np
from jax import lax
from jax.experimental import pallas as pl
from jax.experimental.pallas import tpu as pltpu
from jax.sharding import PartitionSpec as P

MESH = pl.DeviceIdType.MESH
F32 = jnp.float32
CHEB = 8
STEPS = 32
HALF_SPAN = 12.0
NTM, NSP = 16, 8
NDEV = NTM * NSP
OFFSETS = sorted(
    [(dx, dz, dy, dc) for dx in range(4) for dz in range(4) for dy in range(4) for dc in range(2)][1:],
    key=lambda o: -sum(min(d, 4 - d) for d in o[:3]),
)
DEPTH = 4
BLOCK = 4
UNROLL = 8
SIDES = [(-1, 0), (1, 0), (0, -1), (0, 1), (-1, -1), (-1, 1), (1, -1), (1, 1)]


def tables():
    lane = np.arange(128)
    slot, pair = lane // 8, lane % 8
    dft = np.zeros((2, 128, 2, 128))
    back = np.zeros((2, 128, 2, 128))
    same = (pair[:, None] == pair[None, :]).astype(np.float64)
    for half in range(2):
        n = 2 * slot + half
        angle = 2 * np.pi * ((n[:, None] * slot[None, :]) % STEPS) / STEPS
        sign = np.where(n % 2 == 0, 1.0, -1.0)[:, None]
        first = (slot == 0)[None, :]
        real = np.cos(angle)
        imag = np.where(first, sign, -np.sin(angle))
        weight = np.where(first, 1.0, 2.0) / STEPS
        dft[half, :, 0, :] = same * real
        dft[half, :, 1, :] = same * imag
        back[0, :, half, :] = (same * real * weight).T
        back[1, :, half, :] = (same * imag * weight).T
    trig = np.zeros((16, 128))
    for row in range(8):
        freq = np.where((slot == 0) & (row >= 4), 16, slot)
        angle = 2 * np.pi * freq / STEPS
        trig[row] = np.cos(angle)
        trig[8 + row] = np.where(slot == 0, 0.0, np.sin(angle))
    return (
        dft.reshape(256, 256).astype(np.float32),
        back.reshape(256, 256).astype(np.float32),
        trig.astype(np.float32),
    )


def cmul(a, b):
    return (a[0] * b[0] - a[1] * b[1], a[0] * b[1] + a[1] * b[0])


def cinv(a):
    denom = a[0] * a[0] + a[1] * a[1]
    return (a[0] / denom, -a[1] / denom)


def chebyshev_table(log_alpha, cos_f, sin_f):
    ratio = jnp.exp(log_alpha / STEPS)
    center = (1.0 - ratio * cos_f + HALF_SPAN, ratio * sin_f)
    sigma = (center[0] / HALF_SPAN, center[1] / HALF_SPAN)
    rho = [cinv(sigma)]
    for _ in range(CHEB):
        rho.append(cinv((2.0 * sigma[0] - rho[-1][0], 2.0 * sigma[1] - rho[-1][1])))
    inner = (jnp.ones_like(cos_f), jnp.zeros_like(cos_f))
    gains = [None] * (CHEB + 1)
    for j in range(CHEB, -1, -1):
        if j < CHEB:
            step = cmul(cmul(rho[j + 1], rho[j]), inner)
            inner = (1.0 + step[0], step[1])
        scale = cinv(center) if j == 0 else (rho[j][0] / 6.0, rho[j][1] / 6.0)
        gains[j] = cmul(scale, inner)
    level = (jnp.ones_like(cos_f), jnp.zeros_like(cos_f))
    terms = []
    for j in range(CHEB + 1):
        terms.append(cmul(gains[j], level))
        level = cmul(level, rho[j])
    zero = (jnp.zeros_like(cos_f), jnp.zeros_like(cos_f))
    terms += [zero, zero]
    out = []
    for j in range(CHEB + 1):
        own = terms[j] if j == 0 else (0.5 * terms[j][0], 0.5 * terms[j][1])
        out.append((own[0] - 0.5 * terms[j + 2][0], own[1] - 0.5 * terms[j + 2][1]))
    for m in range(BLOCK, 0, -1):
        for j in range(BLOCK + m - 2, BLOCK - m - 1, -2):
            out[j] = (out[j][0] - out[BLOCK + m][0], out[j][1] - out[BLOCK + m][1])
    return out


def swap_groups(a):
    group = lax.broadcasted_iota(jnp.int32, a[0].shape, 1) // 32
    upper = group >= 2
    odd = group % 2 == 1
    c0 = jnp.where(upper, pltpu.roll(a[2], 64, 1), a[0])
    c2 = jnp.where(upper, a[2], pltpu.roll(a[0], 64, 1))
    c1 = jnp.where(upper, pltpu.roll(a[3], 64, 1), a[1])
    c3 = jnp.where(upper, a[3], pltpu.roll(a[1], 64, 1))
    return (
        jnp.where(odd, pltpu.roll(c1, 32, 1), c0),
        jnp.where(odd, c1, pltpu.roll(c0, 96, 1)),
        jnp.where(odd, pltpu.roll(c3, 32, 1), c2),
        jnp.where(odd, c3, pltpu.roll(c2, 96, 1)),
    )


def tile_of(tm, sp):
    cx, cz, cy, core = tm // 4, tm % 4, sp // 2, sp % 2
    zhi = cz // 2
    zlo = (cz + 1) // 2 % 2
    a = cx + zlo * (7 - 2 * cx)
    b = cy + zhi * (7 - 2 * cy)
    return 2 * a + core, b


def device_of(xi, yi):
    a, core = xi // 2, xi % 2
    zlo, zhi = a // 4, yi // 4
    cx = a + zlo * (7 - 2 * a)
    cy = yi + zhi * (7 - 2 * yi)
    cz = zlo + zhi * (3 - 2 * zlo)
    return cx * 4 + cz, cy * 2 + core


def two_terms(a):
    head = a.astype(jnp.bfloat16)
    return head, (a - head.astype(F32)).astype(jnp.bfloat16)


def dot(a, head, rest):
    a_head, a_rest = two_terms(a)
    small = jnp.dot(a_rest, head, preferred_element_type=F32) + jnp.dot(a_head, rest, preferred_element_type=F32)
    return jnp.dot(a_head, head, preferred_element_type=F32) + small


def kernel(
    anum, cond, source_in, start_in, guess_in, classes_in, dft_in, back_in, trig_in, recv2,
    source, start, guess, classes, dft, back, dft0, dft1, back0, back1, trig, insem, send1, recv1, send2a, send2b, cls_send, cls_recv, kap, wxm, wxp, wym, wyp, wzi, wzm, wzp, wc,
    u0, u1, u2, u3, acc, beta, tsem, ksend, krecv, hsend, hrecv, selfsem,
):
    tm = lax.axis_index("tm")
    sp = lax.axis_index("space")
    me = tm * NSP + sp
    xi, yi = tile_of(tm, sp)
    tile = xi * 8 + yi

    planes = [[(tm // 4 + dx) % 4 * 4 + (tm + dz) % 4 for dz in range(4)] for dx in range(4)]
    places = [[(sp // 2 + dy) % 4 * 2 + (sp + dc) % 2 for dc in range(2)] for dy in range(4)]

    zhi = tm % 4 // 2
    half_lanes = pl.ds(pl.multiple_of(zhi * 128, 128), 128)
    pair_rows = pl.ds(pl.multiple_of(xi // 2 * 32, 32), 32)
    pairs = [
        (source_in, source),
        (classes_in.at[:, pair_rows, half_lanes], classes),
        (trig_in, trig),
        (dft_in, dft),
        (back_in, back),
    ]
    loads = [pltpu.make_async_copy(a, b, insem.at[i]) for i, (a, b) in enumerate(pairs)]
    firsts = [
        pltpu.make_async_copy(start_in, start, insem.at[5]),
        pltpu.make_async_copy(guess_in, guess, insem.at[6]),
    ]
    for copy in loads:
        copy.start()

    @pl.when(tm == 0)
    def _():
        for copy in firsts:
            copy.start()


    barrier = pltpu.get_barrier_semaphore()
    for dx, dz, dy, dc in OFFSETS:
        pl.semaphore_signal(barrier, inc=1, device_id=(planes[dx][dz], places[dy][dc]), device_id_type=MESH)

    low_x, high_x, low_y, high_y = xi > 0, xi < 15, yi > 0, yi < 7
    beside = {-1: low_x, 1: high_x}, {-1: low_y, 1: high_y}

    def here(dx, dy):
        if dx and dy:
            return jnp.logical_and(beside[0][dx], beside[1][dy])
        return beside[0][dx] if dx else beside[1][dy]

    def span(d, low, middle, high):
        return {-1: low, 0: middle, 1: high}[d]

    def halo(dx, dy):
        return (
            span(dx, pl.ds(0, DEPTH), pl.ds(DEPTH, 16), pl.ds(DEPTH + 16, DEPTH)),
            span(dy, pl.ds(36, 4), pl.ds(0, 32), pl.ds(32, 4)),
        )

    log_alpha = jnp.log(jnp.full((8, 128), anum[0].astype(F32) / 32.0, F32))
    alpha = anum[0].astype(F32) / 32.0
    n0 = (2 * tm).astype(F32)
    scales = [jnp.exp(log_alpha * (n0 + t) / STEPS) for t in range(2)]

    loads[0].wait()

    @pl.when(tm == 0)
    def _():
        for copy in firsts:
            copy.wait()

        def correct(x, carry):
            rows = pl.ds(pl.multiple_of(x * 16, 16), 16)
            for z in range(2):
                source[0, z, rows, :] = source[0, z, rows, :] + (start[z, rows, :] - alpha * guess[z, rows, :])
            return carry

        lax.fori_loop(0, 16, correct, 0)

    def pack(step, carry):
        todo = []
        for x, xt in [(4 * step + i, xt) for i in range(4) for xt in range(2)]:
            rows = pl.ds(pl.multiple_of(x * 16 + xt * 8, 8), 8)
            for h in range(2):
                lanes = slice(h * 128, h * 128 + 128)
                parts = []
                for t in range(2):
                    for z in range(2):
                        value = source[t, z, rows, lanes]
                        parts.append(value * scales[t])
                for j, value in enumerate(swap_groups(parts)):
                    at = pl.multiple_of((x * 8 + h * 4 + j) * 16 + xt * 8, 8)
                    todo.append((at, value))
        for at, value in todo:
            send1[pl.ds(at, 8), :] = value
        return carry

    lax.fori_loop(0, 4, pack, 0)

    loads[1].wait()
    for core in range(2):
        parts = [
            classes[z, core * 16 + xt * 8 : core * 16 + xt * 8 + 8, :]
            for xt in range(2)
            for z in range(2)
        ]
        for j, value in enumerate(swap_groups(parts)):
            cls_send[core, j] = value

    pl.semaphore_wait(barrier, NDEV - 1)

    def cls_go(k, carry):
        other = (sp + k) % NSP
        ocy, ocore = other // 2, other % 2
        j = ocy + zhi * (3 - 2 * ocy)
        pltpu.make_async_remote_copy(
            src_ref=cls_send.at[ocore, j],
            dst_ref=cls_recv.at[pl.ds(pl.multiple_of(sp * 8, 8), 8)],
            send_sem=tsem.at[4],
            recv_sem=tsem.at[5],
            device_id=(tm, other),
            device_id_type=MESH,
        ).start()
        return carry

    lax.fori_loop(1, NSP, cls_go, 0)

    def rows16(index):
        return pl.ds(pl.multiple_of(index * 16, 16), 16)

    tiles_x = [[tile_of(planes[dx][dz], sp)[0] - sp % 2 for dz in range(4)] for dx in range(4)]
    tiles_y = [[tile_of(planes[0][dz], places[dy][0])[1] for dz in range(4)] for dy in range(4)]
    for dx, dz, dy, dc in OFFSETS:
        other = (tiles_x[dx][dz] + (sp + dc) % 2) * 8 + tiles_y[dy][dz]
        pltpu.make_async_remote_copy(
            src_ref=send1.at[rows16(other)],
            dst_ref=recv1.at[rows16(me)],
            send_sem=tsem.at[0],
            recv_sem=tsem.at[1],
            device_id=(planes[dx][dz], places[dy][dc]),
            device_id_type=MESH,
        ).start()
    recv1[rows16(me), :] = send1[rows16(tile), :]
    mycy, mycore = sp // 2, sp % 2
    cls_recv[pl.ds(pl.multiple_of(sp * 8, 8), 8), :] = cls_send[mycore, mycy + zhi * (3 - 2 * mycy)]

    for copy in loads[2:]:
        copy.wait()
    dft0[...], dft1[...] = two_terms(dft[...])
    back0[...], back1[...] = two_terms(back[...])
    for j, (re, im) in enumerate(chebyshev_table(log_alpha, trig[0:8, :], trig[8:16, :])):
        beta[j, 0:1, :] = re[0:1]
        beta[j, 1:2, :] = im[0:1]
        beta[j, 2:3, :] = -im[0:1]
        beta[j, 3:4, :] = re[4:5]

    for dx, dy in SIDES:

        @pl.when(jnp.logical_not(here(dx, dy)))
        def _(dx=dx, dy=dy):
            xs, ys = halo(dx, dy)
            for ref in (kap, u0.at[0], u0.at[1], u3.at[0], u3.at[1]):
                ref[xs, :, ys, :] = jnp.zeros((xs.size, 2, ys.size, 128), F32)

    some = cls_recv.at[pl.ds(0, 56)]
    pltpu.make_async_copy(some, some, tsem.at[5]).wait()

    def conductivities(xx, carry):
        codes = cls_recv[pl.ds(xx, 8, stride=8), :]
        value = jnp.zeros((8, 128), F32)
        for level in range(8):
            value = jnp.where(codes == level, cond[level], value)
        full = jnp.concatenate([value] * 16, axis=0).T
        for xt in range(2):
            kap[DEPTH + xt * 8 + xx, :, 0:32, :] = full[xt * 64 : xt * 64 + 64].reshape(2, 32, 128)
        return carry

    lax.fori_loop(0, 8, conductivities, 0)

    def edge(dx, dy):
        return (
            span(dx, pl.ds(DEPTH, DEPTH), pl.ds(DEPTH, 16), pl.ds(16, DEPTH)),
            span(dy, pl.ds(0, 4), pl.ds(0, 32), pl.ds(28, 4)),
        )

    def exchange(ref, send, recv, act):
        for i, (dx, dy) in enumerate(SIDES):

            @pl.when(here(dx, dy))
            def _(i=i, dx=dx, dy=dy):
                xs, ys = edge(dx, dy)
                xd, yd = halo(-dx, -dy)
                back_at = SIDES.index((-dx, -dy))
                copy = pltpu.make_async_remote_copy(
                    src_ref=ref.at[xs, :, ys, :],
                    dst_ref=ref.at[xd, :, yd, :],
                    send_sem=send.at[i],
                    recv_sem=recv.at[back_at],
                    device_id=device_of(
                        jnp.clip(xi + dx, 0, 15) if dx else xi, jnp.clip(yi + dy, 0, 7) if dy else yi
                    ),
                    device_id_type=MESH,
                )
                if act == "start":
                    copy.start()
                else:
                    copy.wait_send()
                    xh, yh = halo(dx, dy)
                    got = ref.at[xh, :, yh, :]
                    pltpu.make_async_copy(got, got, recv.at[i]).wait()

    exchange(kap, ksend, krecv, "start")
    most = recv1.at[pl.ds(0, (NDEV - 1) * 16)]
    pltpu.make_async_copy(most, most, tsem.at[1]).wait()

    def forward(quad, carry):
        rows = []
        for i in range(4):
            cells = recv1[pl.ds(quad * 4 + i, 128, stride=16), :].T
            rows.append(jnp.concatenate([cells[:64], cells[64:]], axis=1))
        spectrum = dot(jnp.concatenate(rows, axis=0), dft0[...], dft1[...])
        for i in range(4):
            x = quad * 4 + i
            for z in range(2):
                at = i * 64 + z * 32
                re = spectrum[at : at + 32, 0:128]
                im = spectrum[at : at + 32, 128:256]
                u0[0, DEPTH + x, z, 0:32] = re
                u0[1, DEPTH + x, z, 0:32] = im
                acc[0, x, z] = beta[0, 0:1, :] * re + beta[0, 2:3, :] * im
                acc[1, x, z] = beta[0, 1:2, :] * re + beta[0, 3:4, :] * im
        return carry

    lax.fori_loop(0, 4, forward, 0)

    def swap(block, p, act):
        exchange((u0, u3)[block].at[p], hsend.at[block, p], hrecv.at[block, p], act)

    def chebyshev(block, p, half=None):
        begin = (u0, u3)[block]
        for m in range(BLOCK):
            now = (begin, u1, begin, u2)[m]
            old = (None, begin, u1, begin)[m]
            new = (u1, begin, u2, u3)[m]
            last = m == BLOCK - 1
            spare = BLOCK - 1 - m
            h = slice(0, 32 if last else 40)

            def sweep(first, count, now=now, old=old, new=new, last=last, h=h):
                field = [[now[p, first + i, z] for z in range(2)] for i in range(-1, count + 1)]
                values = []
                for i in range(count):
                    x = first + i
                    below, mid, above = field[i], field[i + 1], field[i + 2]
                    for z in range(2):
                        other = mid[1 - z][h]
                        outer = pltpu.roll(other, 1 if z == 0 else 127, 1)
                        before = pltpu.roll(mid[z], 1, 0)[h]
                        after = pltpu.roll(mid[z], 39, 0)[h]
                        value = wc[x, z, h] * mid[z][h] + wzi[x, h] * other
                        value = value + (wxm[x, z, h] * below[z][h] + wxp[x, z, h] * above[z][h])
                        if old is not None:
                            value = value - old[p, x, z, h]
                        rest = wym[x, z, h] * before + wyp[x, z, h] * after
                        value = value + (rest + (wzm if z == 0 else wzp)[x, h] * outer)
                        values.append((x, z, mid[z][h], value))
                if last:
                    totals = []
                    for x, z, own, value in values:
                        terms = [u1[p, x, z, h], old[p, x, z, h], own, value]
                        for to in range(2):
                            at = 2 * p + to
                            total = beta[BLOCK * block + 1, at : at + 1, :] * terms[0]
                            for i in range(1, 4):
                                total = total + beta[BLOCK * block + 1 + i, at : at + 1, :] * terms[i]
                            totals.append((to, x, z, acc[to, x - DEPTH, z] + total))
                    for to, x, z, total in totals:
                        acc[to, x - DEPTH, z] = total
                if not last or block == 0:
                    for x, z, own, value in values:
                        new[p, x, z, h] = value

            begin_at = DEPTH + 8 + spare if half == 1 else DEPTH - spare
            end_at = DEPTH + 8 + spare if half == 0 else DEPTH + 16 + spare
            steps, rest = divmod(end_at - begin_at, UNROLL)

            def several(step, carry, sweep=sweep, begin_at=begin_at):
                sweep(begin_at + step * UNROLL, UNROLL)
                return carry

            if steps > 1:
                lax.fori_loop(0, steps, several, 0)
            else:
                several(0, 0)
            if rest:
                sweep(begin_at + steps * UNROLL, rest)

    swap(0, 0, "start")
    exchange(kap, ksend, krecv, "wait")

    row_at = lax.broadcasted_iota(jnp.int32, (40, 128), 0)
    pair_at = lax.broadcasted_iota(jnp.int32, (40, 128), 1) % 8
    one = jnp.ones((40, 128), F32)
    inside_low = jnp.where(low_y, 1.0, 0.0).astype(F32)
    inside_high = jnp.where(high_y, 1.0, 0.0).astype(F32)
    columns = jnp.where(row_at < 32, one, jnp.where(row_at < 36, one * inside_high, one * inside_low)) * (1.0 / 12.0)

    def weights(x, carry):
        total = [None, None]
        inside_x = jnp.logical_and(jnp.logical_or(x >= DEPTH, low_x), jnp.logical_or(x < DEPTH + 16, high_x))
        part = columns * jnp.where(inside_x, 1.0, 0.0).astype(F32)
        k = [kap[x, z] for z in range(2)]
        for z in range(2):
            low = (k[z] + kap[x - 1, z]) * part
            high = (k[z] + kap[x + 1, z]) * part
            wxm[x, z] = low
            wxp[x, z] = high
            before = (k[z] + pltpu.roll(k[z], 1, 0)) * part
            after = (k[z] + pltpu.roll(k[z], 39, 0)) * part
            wym[x, z] = before
            wyp[x, z] = after
            total[z] = (low + high) + (before + after)
        inside = (k[0] + k[1]) * part
        below = (k[0] + jnp.where(pair_at == 0, 0.0, pltpu.roll(k[1], 1, 1))) * part
        above = (k[1] + jnp.where(pair_at == 7, 0.0, pltpu.roll(k[0], 127, 1))) * part
        wzi[x] = inside
        wzm[x] = jnp.where(pair_at == 0, 0.0, below)
        wzp[x] = jnp.where(pair_at == 7, 0.0, above)
        wc[x, 0] = part * 24.0 - (total[0] + (inside + below))
        wc[x, 1] = part * 24.0 - (total[1] + (inside + above))
        return carry

    lax.fori_loop(1, 23, weights, 0)
    swap(0, 1, "start")

    for p in range(2):
        swap(0, p, "wait")
        chebyshev(0, p)
        swap(1, p, "start")

    def inverse(quad):
        rows = []
        for i in range(4):
            x = quad * 4 + i
            rows.append(
                jnp.concatenate([acc[0, x].reshape(64, 128), acc[1, x].reshape(64, 128)], axis=1)
            )
        times = dot(jnp.concatenate(rows, axis=0), back0[...], back1[...])
        half_out = send2a if quad < 2 else send2b
        for i in range(4):
            own = times[i * 64 : i * 64 + 64]
            cells = jnp.concatenate([own[:, :128], own[:, 128:]], axis=0)
            half_out[pl.ds(quad % 2 * 4 + i, 128, stride=8), :] = cells.T

    kept = []
    for half, half_out in enumerate((send2a, send2b)):
        for p in range(2):
            if half == 0:
                swap(1, p, "wait")
            chebyshev(1, p, half)
        inverse(2 * half)
        inverse(2 * half + 1)
        mine = pl.ds(pl.multiple_of(tile * 16 + half * 8, 8), 8)
        for dx, dz, dy, dc in OFFSETS:
            to = planes[dx][dz] * NSP + places[dy][dc]
            pltpu.make_async_remote_copy(
                src_ref=half_out.at[pl.ds(pl.multiple_of(to * 8, 8), 8)],
                dst_ref=recv2.at[mine],
                send_sem=tsem.at[2],
                recv_sem=tsem.at[3],
                device_id=(planes[dx][dz], places[dy][dc]),
                device_id_type=MESH,
            ).start()
        stays = pltpu.make_async_copy(half_out.at[pl.ds(pl.multiple_of(me * 8, 8), 8)], recv2.at[mine], selfsem.at[half])
        stays.start()
        kept.append(stays)
    most2 = recv2.at[pl.ds(0, (NDEV - 1) * 16)]
    for stays in kept:
        stays.wait()
    pltpu.make_async_copy(most2, most2, tsem.at[3]).wait()

    pltpu.make_async_copy(most, most, tsem.at[0]).wait()
    pltpu.make_async_copy(most2, most2, tsem.at[2]).wait()
    pltpu.make_async_copy(some, some, tsem.at[4]).wait()


def unpack_kernel(anum, tiles, out):
    log_alpha = jnp.log(jnp.full((8, 128), anum[0].astype(F32) / 32.0, F32))
    n0 = (2 * lax.axis_index("tm")).astype(F32)
    unscales = [jnp.exp(-log_alpha * (n0 + t) / STEPS) for t in range(2)]

    def pair(step, carry):
        todo = []
        for x, xt in [(4 * step + i, xt) for i in range(4) for xt in range(2)]:
            row = pl.multiple_of(x * 16 + xt * 8, 8)
            for h in range(2):
                parts = [
                    tiles[pl.ds(pl.multiple_of((x * 8 + h * 4 + j) * 16 + xt * 8, 8), 8), :] for j in range(4)
                ]
                for i, value in enumerate(swap_groups(parts)):
                    todo.append((i // 2, i % 2, row, h * 128, value * unscales[i // 2]))
        for t, z, row, lane, value in todo:
            out[t, z, pl.ds(row, 8), lane : lane + 128] = value
        return carry

    lax.fori_loop(0, out.shape[2] // 64, pair, 0)


def body(source, start_field, last_guess, classes, conductivity, alpha_num):
    consts = [jnp.asarray(t) for t in tables()]
    smem = pl.BlockSpec(memory_space=pltpu.SMEM)
    hbm = pl.BlockSpec(memory_space=pltpu.HBM)
    BF16 = jnp.bfloat16
    V = pltpu.VMEM
    tiles = pl.pallas_call(
        kernel,
        out_shape=jax.ShapeDtypeStruct((2048, 128), F32),
        in_specs=[smem, smem] + [hbm] * 7,
        out_specs=hbm,
        scratch_shapes=[
            V((2, 2, 256, 256), F32), V((2, 256, 256), F32), V((2, 256, 256), F32), V((2, 32, 128), jnp.int32),
            V((256, 256), F32), V((256, 256), F32), V((256, 256), BF16), V((256, 256), BF16), V((256, 256), BF16), V((256, 256), BF16), V((16, 128), F32),
            pltpu.SemaphoreType.DMA((7,)),
            V((2048, 128), F32), V((2064, 128), F32), V((1032, 128), F32), V((1032, 128), F32),
            V((2, 4, 8, 128), jnp.int32), V((72, 128), jnp.int32),
            V((24, 2, 40, 128), F32), V((24, 2, 40, 128), F32), V((24, 2, 40, 128), F32), V((24, 2, 40, 128), F32),
            V((24, 2, 40, 128), F32),
            V((24, 40, 128), F32), V((24, 40, 128), F32), V((24, 40, 128), F32), V((24, 2, 40, 128), F32),
            V((2, 24, 2, 40, 128), F32), V((2, 24, 2, 40, 128), F32), V((2, 24, 2, 40, 128), F32), V((2, 24, 2, 40, 128), F32), V((2, 16, 2, 32, 128), F32), V((CHEB + 1, 8, 128), F32),
            pltpu.SemaphoreType.DMA((6,)),
            pltpu.SemaphoreType.DMA((8,)), pltpu.SemaphoreType.DMA((8,)),
            pltpu.SemaphoreType.DMA((2, 2, 8)), pltpu.SemaphoreType.DMA((2, 2, 8)), pltpu.SemaphoreType.DMA((2,)),
        ],
        compiler_params=pltpu.CompilerParams(
            collective_id=1, has_side_effects=True, vmem_limit_bytes=62 * 2**20
        ),
    )(alpha_num, conductivity, source, start_field, last_guess, classes, *consts)
    steps = 2
    return pl.pallas_call(
        unpack_kernel,
        grid=(steps,),
        out_shape=jax.ShapeDtypeStruct((2, 2, 256, 256), F32),
        in_specs=[smem, pl.BlockSpec((2048 // steps, 128), lambda i: (i, 0))],
        out_specs=pl.BlockSpec((2, 2, 256 // steps, 256), lambda i: (0, 0, i, 0)),
    )(alpha_num, tiles)


def solution(mesh):
    placed = (
        P("tm", "space", None, None),
        P("space", None, None),
        P("space", None, None),
        P("space", None, None),
        P(),
        P(),
    )
    return jax.shard_map(
        body, mesh=mesh, in_specs=placed, out_specs=P("tm", "space", None, None), check_vma=False
    )
```
